128 devices in a mesh: row: 8 (over y, core), col: 16 (over z, x).
Axes of the slice: x: 4, y: 4, z: 4, core: 2. Of those that a mesh axis runs over, the one named last changes fastest.
Arguments:
- blocks: bfloat16 [512, 10, 256, 256], P(('row', 'col')), may hold values from -0.0625 to 0.0625
- block_scales: float32 [512, 10], P(('row', 'col')), may hold values from 0.15 to 0.6
- columns: int32 [512, 10], P(('row', 'col')), may hold values from 0 to 511, as said below
- live: int32 [512], P(('row', 'col')), may hold values from 3 to 10
- onsite: float32 [131072], P(('row', 'col')), may hold values from -1 to 1
- start_vectors: bfloat16 [131072, 128], P(('row', 'col')), may hold values from -6 to 6
Outputs:
- basis: float32 [131072, 128], P(('row', 'col'))
The draws below stay inside these ranges and needn't reach their ends.
Inputs may be any that keep to these rules, and one draw needn't show every extreme that they name: `columns`: slot 0 of each block row is the row itself; every column lies within 4 block rows of its row, cyclically over 512, and that distance is reached in both directions in every draw.
All inputs are finite; a program needn't handle non-finite values.
Results may differ from the reference program's by a relative error of at most 0.014.
Values may be sent and summed in bfloat16 or wider, within the bound.
No kernel may reach another device: no remote copies, remote signals or barrier semaphores. Data moves between devices by JAX's collectives and lax.ppermute only.
A program may use at most 128 MiB of HBM per device.

```python
import math
import jax
import jax.numpy as jnp
from jax import lax

BLOCK = 256
K = 128
NBR = 10
DEG = 5
BR_DEV = 4
NB = 512
ORDER = 131072


def draw_columns(key, part):
    key = jax.random.fold_in(key, 7)
    rows = jnp.arange(NB, dtype=jnp.int32)
    offsets = jax.random.randint(key, (NB, NBR - 1), -BR_DEV, BR_DEV + 1).astype(jnp.int32)
    marked = rows % BR_DEV == 0
    offsets = offsets.at[:, 0].set(jnp.where(marked, BR_DEV, offsets[:, 0]))
    offsets = offsets.at[:, 1].set(jnp.where(marked, -BR_DEV, offsets[:, 1]))
    others = (rows[:, None] + offsets) % NB
    return jnp.concatenate([rows[:, None], others], axis=1).astype(jnp.int32)


def with_ends(array, rng, least, top_value):
    place = [jax.random.randint(jax.random.fold_in(rng, axis), (), 0, length) for axis, length in enumerate(array.shape)]
    main_axis = array.shape.index(max(array.shape))
    beside = place[:main_axis] + [(place[main_axis] + 1) % array.shape[main_axis]] + place[main_axis + 1:]
    return array.at[tuple(place)].set(least).at[tuple(beside)].set(top_value)


def block_levels(own_key, extent, shards, low, largest):
    gain, own = 1.0, jax.random.fold_in(own_key, 6)
    for position, parts in shards:
        draws = jnp.exp(jax.random.uniform(jax.random.fold_in(own, position), (parts,), jnp.float32, low / len(shards), largest / len(shards)))
        gain = gain * jnp.repeat(draws, extent[position] // parts).reshape([-1 if axis == position else 1 for axis in range(len(extent))])
    return gain


def centred(own_key, dims, scale, most, cuts=(), kind=jnp.bfloat16):
    level = block_levels(own_key, dims, cuts, -0.22, 0.18) if cuts else 1.0
    values = jax.random.normal(own_key, dims, jnp.float32) * scale * level
    return jnp.minimum(jnp.maximum(values, -most), most).astype(kind)


def setup_inputs(seed: int = 0) -> dict:
    keys = jax.random.split(jax.random.key(seed), 7)
    return {
        "blocks": centred(keys[0], (NB, NBR, BLOCK, BLOCK), (4 * BLOCK * NBR) ** -0.5, 0.0625, ((0, 128),)),
        "block_scales": jnp.clip(jnp.exp(math.log(0.6) - 1.3862944 * jax.random.uniform(keys[1], (NB, NBR), jnp.float32) ** block_levels(keys[1], (NB, NBR), ((0, 128),), -0.2, 0.2)), 0.15, 0.6),
        "columns": draw_columns(jax.random.fold_in(keys[6], 71), 0),
        "live": with_ends(jax.random.randint(keys[3], (NB,), 3, NBR + 1), jax.random.fold_in(keys[3], 1), 3, NBR).astype(jnp.int32),
        "onsite": jnp.clip(jax.random.uniform(keys[4], (ORDER,), jnp.float32, -1.0, 1.0) * block_levels(keys[4], (ORDER,), ((0, 128),), -0.4, 0.0), -1.0, 1.0),
        "start_vectors": centred(keys[5], (ORDER, K), 1.0, 6.0, ((0, 128),)),
    }


def apply_ham(vecs, blocks, block_scales, columns, live, onsite):
    tall = vecs.reshape(NB, BLOCK, K)
    slot_index = jnp.arange(NBR, dtype=jnp.int32)
    weights = block_scales * (slot_index[None, :] < live[:, None]).astype(jnp.float32)
    groups = NB // BR_DEV
    starts = jnp.arange(groups, dtype=jnp.int32) * BR_DEV

    def one_group(acc, args):
        blk, wgt, cols, first = args
        blk32 = blk.astype(jnp.float32)
        picked = tall[cols].astype(jnp.float32)
        prods = jnp.einsum('rsij,rsjk->rsik', blk32, picked, precision=lax.Precision.HIGHEST)
        forward = jnp.einsum('rs,rsik->rik', wgt, prods, precision=lax.Precision.HIGHEST)
        own = lax.dynamic_slice_in_dim(tall, first, BR_DEV, 0).astype(jnp.float32)
        back = jnp.einsum('rsji,rjk->rsik', blk32, own, precision=lax.Precision.HIGHEST)
        back = back * wgt[:, :, None, None]
        acc = acc.at[cols.reshape(-1)].add(back.reshape(BR_DEV * NBR, BLOCK, K))
        return (acc, forward)
    acc0 = jnp.zeros((NB, BLOCK, K), jnp.float32)
    acc, out = lax.scan(one_group, acc0, (blocks.reshape(groups, BR_DEV, NBR, BLOCK, BLOCK), weights.reshape(groups, BR_DEV, NBR), columns.reshape(groups, BR_DEV, NBR), starts))
    return (out.reshape(NB, BLOCK, K) + acc).reshape(ORDER, K) + onsite[:, None] * vecs.astype(jnp.float32)

def reference(blocks, block_scales, columns, live, onsite, start_vectors):
    older = start_vectors
    image = apply_ham(older, blocks, block_scales, columns, live, onsite)
    newer = ((image - 0.2 * older.astype(jnp.float32)) / 1.1).astype(jnp.bfloat16)
    for step in range(DEG - 1):
        image = apply_ham(newer, blocks, block_scales, columns, live, onsite)
        nxt = (2.0 * (image - 0.2 * newer.astype(jnp.float32)) / 1.1 - older.astype(jnp.float32)).astype(jnp.bfloat16)
        older, newer = (newer, nxt)
    gram = lax.dot_general(newer.astype(jnp.float32), newer.astype(jnp.float32), (((0,), (0,)), ((), ())), preferred_element_type=jnp.float32)
    lower = jnp.linalg.cholesky(gram)
    solved_block = lax.linalg.triangular_solve(lower, newer.astype(jnp.float32), left_side=False, lower=True, transpose_a=True)
    return solved_block * jnp.sqrt(jnp.float32(ORDER))
```

```python
import jax
import jax.numpy as jnp
from jax import lax
from jax.experimental import pallas as pl
from jax.experimental.pallas import tpu as pltpu
from jax.sharding import PartitionSpec as P

DEG = 5
B = 256
K = 128
ROWS = 4
OWN = ROWS * B
REACH = 4
SPAN = 2 * REACH + 1
AXES = ("row", "col")
ALPHA = 2.0 / 1.1
SHIFT = 0.2
F32 = jnp.float32
BF16 = jnp.bfloat16
EDGE = (8, 9, 2, 3)
TO_RIGHT = ((2, 10), (3, 10), (3, 11))
TO_LEFT = ((0, 0), (0, 1), (1, 1))
HANDED = 3 * 2 * B


def rows(i, n=1):
    return pl.ds(i * B, n * B)


def dot(a, b):
    return jnp.dot(a, b, preferred_element_type=F32)


def read_block(ref, i):
    return jnp.concatenate([ref[rows(2 * i), :], ref[rows(2 * i + 1), :]], axis=1)


def flip(block):
    return block.astype(F32).T


def prep_kernel(weight, offset, live, blocks, y0, own, edge, to_right, to_left, buf, acc, sem):
    copies = [pltpu.make_async_copy(blocks.at[a], buf.at[a], sem.at[a]) for a in range(ROWS)]
    for copy in copies:
        copy.start()
    for a in range(ROWS):
        acc[...] = jnp.zeros_like(acc)
        copies[a].wait()

        def add_slot(s, carry, a=a):
            o = offset[a, s]
            acc[o] = acc[o] + weight[a, s] * buf[a, s].astype(F32)
            return carry

        lax.fori_loop(0, live[a], add_slot, 0)
        for o in range(SPAN):
            p = a + o
            value = acc[o].astype(BF16)
            if 4 <= p < 8:
                own[rows(a), rows(p - 4)] = value
            elif p in EDGE:
                edge[rows(a), rows(EDGE.index(p))] = value
            else:
                places, target = (TO_RIGHT, to_right) if p > 8 else (TO_LEFT, to_left)
                i = places.index((a, p))
                target[rows(2 * i), :] = value[:, :K]
                target[rows(2 * i + 1), :] = value[:, K:]
    edge[rows(0), rows(1)] = jnp.zeros((B, B), BF16)
    edge[rows(3), rows(2)] = jnp.zeros((B, B), BF16)
    turned = flip(y0[...]).astype(BF16)
    terms = dot(turned, edge[...]).T.astype(BF16)
    to_right[pl.ds(HANDED, 2 * B), :] = terms[: 2 * B]
    to_left[pl.ds(HANDED, 2 * B), :] = terms[2 * B :]


def first_local_kernel(own, edge, diag, y0, left, right, to_right, to_left, sym, edge_t, base):
    for a in range(ROWS):
        for b in range(a + 1):
            value = own[rows(a), rows(b)].astype(F32) + flip(own[rows(b), rows(a)])
            sym[rows(a), rows(b)] = value.astype(BF16)
            if b < a:
                sym[rows(b), rows(a)] = value.T.astype(BF16)
    for a in range(ROWS):
        for j in range(4):
            edge_t[rows(j), rows(a)] = flip(edge[rows(a), rows(j)]).astype(BF16)
    base[...] = diag[...] * y0[...].astype(F32) + dot(sym[...], y0[...])
    for places, source, halo, first in ((TO_LEFT, to_left, left, 0), (TO_RIGHT, to_right, right, 8)):
        for i, (a, p) in enumerate(places):
            base[rows(a), :] += dot(read_block(source, i), halo[rows(p - first), :])


def send_parts(y, terms, send_right, send_left):
    send_right[pl.ds(0, 2 * B), :] = y[2 * B :]
    send_right[pl.ds(2 * B, 2 * B), :] = terms[: 2 * B]
    send_left[pl.ds(0, 2 * B), :] = y[: 2 * B]
    send_left[pl.ds(2 * B, 2 * B), :] = terms[2 * B :]


def first_post_kernel(base, edge_in, edge_t_in, left, right, got_left, got_right, edge, edge_t, y_out, send_right, send_left):
    edge[...] = edge_in[...]
    edge_t[...] = edge_t_in[...]
    for i, (r, c) in enumerate(TO_LEFT):
        block = read_block(got_right, i).astype(F32)
        edge_t[rows(r), rows(c)] = (edge_t[rows(r), rows(c)].astype(F32) + block).astype(BF16)
        edge[rows(c), rows(r)] = (edge[rows(c), rows(r)].astype(F32) + block.T).astype(BF16)
    for i, (c, p) in enumerate(TO_RIGHT):
        block = read_block(got_left, i).astype(F32)
        r = p - 8
        edge_t[rows(c), rows(r)] = (edge_t[rows(c), rows(r)].astype(F32) + block).astype(BF16)
        edge[rows(r), rows(c)] = (edge[rows(r), rows(c)].astype(F32) + block.T).astype(BF16)
    halo = jnp.concatenate([right[pl.ds(0, 2 * B), :], left[pl.ds(2 * B, 2 * B), :]], axis=0)
    terms = jnp.concatenate([got_left[pl.ds(HANDED, 2 * B), :], got_right[pl.ds(HANDED, 2 * B), :]], axis=0)
    total = base[...] + dot(edge[...], halo) + terms.astype(F32)
    y = (0.5 * total).astype(BF16)
    y_out[...] = y
    send_parts(y, dot(edge_t[...], y).astype(BF16), send_right, send_left)


def received(base, edge, got_left, got_right):
    halo = jnp.concatenate([got_right[pl.ds(0, 2 * B), :], got_left[pl.ds(0, 2 * B), :]], axis=0)
    terms = jnp.concatenate([got_left[pl.ds(2 * B, 2 * B), :], got_right[pl.ds(2 * B, 2 * B), :]], axis=0)
    return (base[...] + dot(edge[...], halo) + terms.astype(F32)).astype(BF16)


def post_kernel(base, edge, edge_t, got_left, got_right, y_out, send_right, send_left):
    y = received(base, edge, got_left, got_right)
    y_out[...] = y
    send_parts(y, dot(edge_t[...], y).astype(BF16), send_right, send_left)


def last_kernel(base, edge, got_left, got_right, y_out, gram):
    y = received(base, edge, got_left, got_right)
    y_out[...] = y
    gram[...] = lax.dot_general(y, y, (((0,), (0,)), ((), ())), preferred_element_type=F32)


def local_kernel(sym, diag, y, older, base):
    base[...] = diag[...] * y[...].astype(F32) - older[...].astype(F32) + dot(sym[...], y[...])


VMEM = pl.BlockSpec(memory_space=pltpu.VMEM)
SMEM = pl.BlockSpec(memory_space=pltpu.SMEM)
ANY = pl.BlockSpec(memory_space=pl.ANY)
LIMIT = 32 * 1024 * 1024


def call(kernel, outs, specs, flops, size, scratch=(), aliases=None):
    return pl.pallas_call(
        kernel,
        out_shape=[jax.ShapeDtypeStruct(*out) for out in outs],
        in_specs=list(specs),
        out_specs=[VMEM] * len(outs),
        scratch_shapes=list(scratch),
        input_output_aliases=aliases or {},
        cost_estimate=pl.CostEstimate(flops=flops, bytes_accessed=size, transcendentals=0),
        compiler_params=pltpu.CompilerParams(vmem_limit_bytes=LIMIT),
    )


def ring(value, step):
    count = lax.axis_size(AXES)
    return lax.ppermute(value, AXES, [(i, (i + step) % count) for i in range(count)])


def group_sum(value, stride, size):
    count = lax.axis_size(AXES)
    parts = [value]
    for step in range(1, size):
        pairs = []
        for i in range(count):
            digit = (i // stride) % size
            pairs.append((i, i + ((digit + step) % size - digit) * stride))
        parts.append(lax.ppermute(value, AXES, pairs))
    return sum(parts[1:], parts[0])


def digits():
    out, stride = [], 1
    for axis, cut in (("col", 4), ("row", 2)):
        left = lax.axis_size(axis)
        while left > 1:
            size = cut if left % cut == 0 else left
            out.append((stride, size))
            stride *= size
            left //= size
            cut = left if axis == "row" else cut
    return out


def local(blocks, block_scales, columns, live, onsite, start_vectors):
    slots = columns.shape[1]
    total = ROWS * lax.axis_size(AXES)
    row_ids = lax.axis_index(AXES) * ROWS + jnp.arange(ROWS, dtype=jnp.int32)
    offset = (columns - row_ids[:, None] + REACH) % total
    weight = block_scales * ALPHA
    diag = (ALPHA * (onsite - SHIFT))[:, None]
    tall = ((OWN, K), BF16)
    tall32 = ((OWN, K), F32)
    square = ((OWN, OWN), BF16)
    handed = ((HANDED + 2 * B, K), BF16)
    product = 2 * OWN * OWN * K

    y0 = start_vectors
    left, right = ring(y0, 1), ring(y0, -1)
    own, edge, to_right, to_left = call(
        prep_kernel,
        [square, square, handed, handed],
        [SMEM, SMEM, SMEM, ANY, VMEM],
        product,
        10_000_000,
        [
            pltpu.VMEM((ROWS, slots, B, B), BF16),
            pltpu.VMEM((SPAN, B, B), F32),
            pltpu.SemaphoreType.DMA((ROWS,)),
        ],
    )(weight, offset, live, blocks, y0)
    got_left, got_right = ring(to_right, 1), ring(to_left, -1)
    sym, edge_t, base = call(first_local_kernel, [square, square, tall32], [VMEM] * 8, product, 10_000_000)(
        own, edge, diag, y0, left, right, to_right, to_left
    )
    edge, edge_t, y, send_right, send_left = call(
        first_post_kernel, [square, square, tall, tall, tall], [VMEM] * 7, 2 * product, 9_000_000, (), {1: 0, 2: 1}
    )(base, edge, edge_t, left, right, got_left, got_right)
    older = y0
    for step in range(1, DEG):
        got_left, got_right = ring(send_right, 1), ring(send_left, -1)
        base = call(local_kernel, [tall32], [VMEM] * 4, product, 3_500_000)(sym, diag, y, older)[0]
        older = y
        if step < DEG - 1:
            y, send_right, send_left = call(post_kernel, [tall, tall, tall], [VMEM] * 5, 2 * product, 6_000_000)(
                base, edge, edge_t, got_left, got_right
            )
        else:
            y, gram = call(last_kernel, [tall, ((K, K), F32)], [VMEM] * 4, product, 4_000_000)(
                base, edge, got_left, got_right
            )
    for stride, size in digits():
        gram = group_sum(gram, stride, size)
    lower = jnp.linalg.cholesky(gram)
    solved = lax.linalg.triangular_solve(lower, y.astype(F32), left_side=False, lower=True, transpose_a=True)
    return solved * jnp.sqrt(F32(total * B))


def solution(mesh):
    return jax.shard_map(
        local,
        mesh=mesh,
        in_specs=(
            P(AXES, None, None, None),
            P(AXES, None),
            P(AXES, None),
            P(AXES),
            P(AXES),
            P(AXES, None),
        ),
        out_specs=P(AXES, None),
        check_vma=False,
    )
```

```python
import functools

import jax
import jax.numpy as jnp
import numpy as np
from jax import lax
from jax.experimental import pallas as pl
from jax.experimental.pallas import tpu as pltpu
from jax.sharding import PartitionSpec as P

DEG = 5
B = 256
K = 128
ROWS = 4
OWN = ROWS * B
REACH = 4
SPAN = 2 * REACH + 1
AXES = ("row", "col")
ALPHA = 2.0 / 1.1
SHIFT = 0.2
F32 = jnp.float32
BF16 = jnp.bfloat16
EDGE = (8, 9, 2, 3)
TO_RIGHT = ((2, 10), (3, 10), (3, 11))
TO_LEFT = ((0, 0), (0, 1), (1, 1))
HANDED = 3 * 2 * B
T = 8


def rows(i, n=1):
    return pl.ds(i * B, n * B)


def dot(a, b):
    return jnp.dot(a, b, preferred_element_type=F32)


def read_block(ref, i):
    return jnp.concatenate([ref[rows(2 * i), :], ref[rows(2 * i + 1), :]], axis=1)


def flip(block):
    return block.astype(F32).T


def prep_kernel(weight, offset, live, blocks, y0, own, edge, to_right, to_left, buf, acc, sem):
    copies = [pltpu.make_async_copy(blocks.at[a], buf.at[a], sem.at[a]) for a in range(ROWS)]
    for copy in copies:
        copy.start()
    for a in range(ROWS):
        acc[...] = jnp.zeros_like(acc)
        copies[a].wait()

        def add_slot(s, carry, a=a):
            o = offset[a, s]
            acc[o] = acc[o] + weight[a, s] * buf[a, s].astype(F32)
            return carry

        lax.fori_loop(0, live[a], add_slot, 0)
        for o in range(SPAN):
            p = a + o
            value = acc[o].astype(BF16)
            if 4 <= p < 8:
                own[rows(a), rows(p - 4)] = value
            elif p in EDGE:
                edge[rows(a), rows(EDGE.index(p))] = value
            else:
                places, target = (TO_RIGHT, to_right) if p > 8 else (TO_LEFT, to_left)
                i = places.index((a, p))
                target[rows(2 * i), :] = value[:, :K]
                target[rows(2 * i + 1), :] = value[:, K:]
    edge[rows(0), rows(1)] = jnp.zeros((B, B), BF16)
    edge[rows(3), rows(2)] = jnp.zeros((B, B), BF16)
    turned = flip(y0[...]).astype(BF16)
    terms = dot(turned, edge[...]).T.astype(BF16)
    to_right[pl.ds(HANDED, 2 * B), :] = terms[: 2 * B]
    to_left[pl.ds(HANDED, 2 * B), :] = terms[2 * B :]


def first_local_kernel(own, edge, diag, y0, left, right, to_right, to_left, sym, edge_t, base):
    for a in range(ROWS):
        for b in range(a + 1):
            value = own[rows(a), rows(b)].astype(F32) + flip(own[rows(b), rows(a)])
            sym[rows(a), rows(b)] = value.astype(BF16)
            if b < a:
                sym[rows(b), rows(a)] = value.T.astype(BF16)
    for a in range(ROWS):
        for j in range(4):
            edge_t[rows(j), rows(a)] = flip(edge[rows(a), rows(j)]).astype(BF16)
    base[...] = diag[...] * y0[...].astype(F32) + dot(sym[...], y0[...])
    for places, source, halo, first in ((TO_LEFT, to_left, left, 0), (TO_RIGHT, to_right, right, 8)):
        for i, (a, p) in enumerate(places):
            base[rows(a), :] += dot(read_block(source, i), halo[rows(p - first), :])


def send_parts(y, terms, send_right, send_left):
    send_right[pl.ds(0, 2 * B), :] = y[2 * B :]
    send_right[pl.ds(2 * B, 2 * B), :] = terms[: 2 * B]
    send_left[pl.ds(0, 2 * B), :] = y[: 2 * B]
    send_left[pl.ds(2 * B, 2 * B), :] = terms[2 * B :]


def first_post_kernel(base, edge_in, edge_t_in, left, right, got_left, got_right, edge, edge_t, y_out, send_right, send_left):
    edge[...] = edge_in[...]
    edge_t[...] = edge_t_in[...]
    for i, (r, c) in enumerate(TO_LEFT):
        block = read_block(got_right, i).astype(F32)
        edge_t[rows(r), rows(c)] = (edge_t[rows(r), rows(c)].astype(F32) + block).astype(BF16)
        edge[rows(c), rows(r)] = (edge[rows(c), rows(r)].astype(F32) + block.T).astype(BF16)
    for i, (c, p) in enumerate(TO_RIGHT):
        block = read_block(got_left, i).astype(F32)
        r = p - 8
        edge_t[rows(c), rows(r)] = (edge_t[rows(c), rows(r)].astype(F32) + block).astype(BF16)
        edge[rows(r), rows(c)] = (edge[rows(r), rows(c)].astype(F32) + block.T).astype(BF16)
    halo = jnp.concatenate([right[pl.ds(0, 2 * B), :], left[pl.ds(2 * B, 2 * B), :]], axis=0)
    terms = jnp.concatenate([got_left[pl.ds(HANDED, 2 * B), :], got_right[pl.ds(HANDED, 2 * B), :]], axis=0)
    total = base[...] + dot(edge[...], halo) + terms.astype(F32)
    y = (0.5 * total).astype(BF16)
    y_out[...] = y
    send_parts(y, dot(edge_t[...], y).astype(BF16), send_right, send_left)


def received(base, edge, got_left, got_right):
    halo = jnp.concatenate([got_right[pl.ds(0, 2 * B), :], got_left[pl.ds(0, 2 * B), :]], axis=0)
    terms = jnp.concatenate([got_left[pl.ds(2 * B, 2 * B), :], got_right[pl.ds(2 * B, 2 * B), :]], axis=0)
    return (base[...] + dot(edge[...], halo) + terms.astype(F32)).astype(BF16)


def post_kernel(base, edge, edge_t, got_left, got_right, y_out, send_right, send_left):
    y = received(base, edge, got_left, got_right)
    y_out[...] = y
    send_parts(y, dot(edge_t[...], y).astype(BF16), send_right, send_left)


def last_kernel(base, edge, got_left, got_right, y_out, gram):
    y = received(base, edge, got_left, got_right)
    y_out[...] = y
    gram[...] = lax.dot_general(y, y, (((0,), (0,)), ((), ())), preferred_element_type=F32)


def local_kernel(sym, diag, y, older, base):
    base[...] = diag[...] * y[...].astype(F32) - older[...].astype(F32) + dot(sym[...], y[...])


def lane_fill(x, c):
    return jnp.take_along_axis(x, jnp.full((T, K), c, jnp.int32), axis=1)


def row_fill(x, j):
    return jnp.take_along_axis(x, jnp.full((T, K), j, jnp.int32), axis=0)


def inverse_factor(gram, inverse):
    count = K // T
    lane = lax.broadcasted_iota(jnp.int32, (T, K), 1)
    sub = lax.broadcasted_iota(jnp.int32, (T, K), 0)
    tiles = [gram[pl.ds(T * t, T), :] for t in range(count)]
    for k in range(count):
        first = T * k
        inside = (lane >= first) & (lane < first + T)
        spread = [lane_fill(tiles[k], first + c) for c in range(T)]
        rest = jnp.where(inside, 0.0, tiles[k])
        steps = []
        scale = jnp.zeros((T, K), F32)
        for j in range(T):
            pivot = row_fill(spread[j], j)
            inv = 1.0 / pivot
            ratios = {c: row_fill(spread[c], j) * inv for c in range(j + 1, T)}
            row = jnp.where(lane == first + j, 1.0, row_fill(rest, j)) * inv
            steps.append((ratios, row))
            rest = rest - jnp.where(sub > j, spread[j], 0.0) * row
            for c in range(j + 1, T):
                spread[c] = spread[c] - spread[j] * ratios[c]
            scale = jnp.where(sub == j, lax.rsqrt(pivot), scale)
        unit = jnp.where(lane < first + sub, rest, jnp.where(lane == first + sub, 1.0, 0.0))
        inverse[pl.ds(first, T), :] = unit * scale
        for t in range(k + 1, count):
            factors = [lane_fill(tiles[t], first + c) for c in range(T)]
            value = jnp.where(inside, 0.0, tiles[t])
            for j, (ratios, row) in enumerate(steps):
                value = value - factors[j] * row
                for c in range(j + 1, T):
                    factors[c] = factors[c] - factors[j] * ratios[c]
            tiles[t] = value


def finish_kernel(scale, gram, y, basis, inverse):
    inverse_factor(gram, inverse)
    value = inverse[...] * scale
    high = value.astype(BF16)
    low = (value - high.astype(F32)).astype(BF16)
    dims = (((1,), (1,)), ((), ()))
    basis[...] = lax.dot_general(y[...], high, dims, preferred_element_type=F32) + lax.dot_general(
        y[...], low, dims, preferred_element_type=F32
    )


VMEM = pl.BlockSpec(memory_space=pltpu.VMEM)
SMEM = pl.BlockSpec(memory_space=pltpu.SMEM)
ANY = pl.BlockSpec(memory_space=pl.ANY)
LIMIT = 32 * 1024 * 1024


def call(kernel, outs, specs, flops, size, scratch=(), aliases=None):
    return pl.pallas_call(
        kernel,
        out_shape=[jax.ShapeDtypeStruct(*out) for out in outs],
        in_specs=list(specs),
        out_specs=[VMEM] * len(outs),
        scratch_shapes=list(scratch),
        input_output_aliases=aliases or {},
        cost_estimate=pl.CostEstimate(flops=flops, bytes_accessed=size, transcendentals=0),
        compiler_params=pltpu.CompilerParams(vmem_limit_bytes=LIMIT),
    )


def ring(value, step):
    count = lax.axis_size(AXES)
    return lax.ppermute(value, AXES, [(i, (i + step) % count) for i in range(count)])


def group_sum(value, stride, size):
    count = lax.axis_size(AXES)
    parts = [value]
    for step in range(1, size):
        pairs = []
        for i in range(count):
            digit = (i // stride) % size
            pairs.append((i, i + ((digit + step) % size - digit) * stride))
        parts.append(lax.ppermute(value, AXES, pairs))
    return sum(parts[1:], parts[0])


def digits():
    out, stride = [], 1
    for axis, cut in (("col", 4), ("row", 2)):
        left = lax.axis_size(axis)
        while left > 1:
            size = cut if left % cut == 0 else left
            out.append((stride, size))
            stride *= size
            left //= size
            cut = left if axis == "row" else cut
    return out


def local(blocks, block_scales, columns, live, onsite, start_vectors):
    slots = columns.shape[1]
    total = ROWS * lax.axis_size(AXES)
    row_ids = lax.axis_index(AXES) * ROWS + jnp.arange(ROWS, dtype=jnp.int32)
    offset = (columns - row_ids[:, None] + REACH) % total
    weight = block_scales * ALPHA
    diag = (ALPHA * (onsite - SHIFT))[:, None]
    tall = ((OWN, K), BF16)
    tall32 = ((OWN, K), F32)
    square = ((OWN, OWN), BF16)
    handed = ((HANDED + 2 * B, K), BF16)
    product = 2 * OWN * OWN * K

    y0 = start_vectors
    left, right = ring(y0, 1), ring(y0, -1)
    own, edge, to_right, to_left = call(
        prep_kernel,
        [square, square, handed, handed],
        [SMEM, SMEM, SMEM, ANY, VMEM],
        product,
        10_000_000,
        [
            pltpu.VMEM((ROWS, slots, B, B), BF16),
            pltpu.VMEM((SPAN, B, B), F32),
            pltpu.SemaphoreType.DMA((ROWS,)),
        ],
    )(weight, offset, live, blocks, y0)
    got_left, got_right = ring(to_right, 1), ring(to_left, -1)
    sym, edge_t, base = call(first_local_kernel, [square, square, tall32], [VMEM] * 8, product, 10_000_000)(
        own, edge, diag, y0, left, right, to_right, to_left
    )
    edge, edge_t, y, send_right, send_left = call(
        first_post_kernel, [square, square, tall, tall, tall], [VMEM] * 7, 2 * product, 9_000_000, (), {1: 0, 2: 1}
    )(base, edge, edge_t, left, right, got_left, got_right)
    older = y0
    for step in range(1, DEG):
        got_left, got_right = ring(send_right, 1), ring(send_left, -1)
        base = call(local_kernel, [tall32], [VMEM] * 4, product, 3_500_000)(sym, diag, y, older)[0]
        older = y
        if step < DEG - 1:
            y, send_right, send_left = call(post_kernel, [tall, tall, tall], [VMEM] * 5, 2 * product, 6_000_000)(
                base, edge, edge_t, got_left, got_right
            )
        else:
            y, gram = call(last_kernel, [tall, ((K, K), F32)], [VMEM] * 4, product, 4_000_000)(
                base, edge, got_left, got_right
            )
    for stride, size in digits():
        gram = group_sum(gram, stride, size)
    scale = float(np.sqrt(total * B))
    return call(
        functools.partial(finish_kernel, scale), [tall32], [VMEM] * 2, 2 * product, 1_000_000, [pltpu.VMEM((K, K), F32)]
    )(gram, y)[0]


def solution(mesh):
    return jax.shard_map(
        local,
        mesh=mesh,
        in_specs=(
            P(AXES, None, None, None),
            P(AXES, None),
            P(AXES, None),
            P(AXES),
            P(AXES),
            P(AXES, None),
        ),
        out_specs=P(AXES, None),
        check_vma=False,
    )
```

```python
import functools

import jax
import jax.numpy as jnp
import numpy as np
from jax import lax
from jax.experimental import pallas as pl
from jax.experimental.pallas import tpu as pltpu
from jax.sharding import PartitionSpec as P

DEG = 5
B = 256
K = 128
ROWS = 4
OWN = ROWS * B
REACH = 4
SPAN = 2 * REACH + 1
AXES = ("row", "col")
ALPHA = 2.0 / 1.1
SHIFT = 0.2
F32 = jnp.float32
BF16 = jnp.bfloat16
EDGE = (8, 9, 2, 3)
TO_RIGHT = ((2, 10), (3, 10), (3, 11))
TO_LEFT = ((0, 0), (0, 1), (1, 1))
HANDED = 3 * 2 * B
T = 8


def rows(i, n=1):
    return pl.ds(i * B, n * B)


def dot(a, b):
    return jnp.dot(a, b, preferred_element_type=F32)


def read_block(ref, i):
    return jnp.concatenate([ref[rows(2 * i), :], ref[rows(2 * i + 1), :]], axis=1)


def flip(block):
    return block.astype(F32).T


def prep_kernel(total, scales, columns, live, blocks, y0, own, edge, to_right, to_left, buf, acc, head, after, sem):
    copies = [pltpu.make_async_copy(blocks.at[a], buf.at[a], sem.at[a]) for a in range(ROWS)]
    for copy in copies:
        copy.start()
    first = lax.axis_index(AXES) * ROWS
    for a in range(ROWS):
        for o in range(SPAN):
            head[a, o] = -1

        def chain(s, carry, a=a):
            o = lax.rem(columns[a, s] - (first + a) + REACH + total, total)
            after[a, s] = head[a, o]
            head[a, o] = s
            return carry

        lax.fori_loop(0, live[a], chain, 0)
    turned = flip(y0[...]).astype(BF16)
    for target in (to_right, to_left):
        target[pl.ds(HANDED + 2 * B, OWN), :] = y0[...]

    def put(a, p, value):
        if 4 <= p < 8:
            own[rows(a), rows(p - 4)] = value
        elif p in EDGE:
            edge[rows(a), rows(EDGE.index(p))] = value
        else:
            places, target = (TO_RIGHT, to_right) if p > 8 else (TO_LEFT, to_left)
            i = places.index((a, p))
            target[rows(2 * i), :] = value[:, :K]
            target[rows(2 * i + 1), :] = value[:, K:]

    def scaled(a, s):
        return (scales[a, s] * ALPHA) * buf[a, s].astype(F32)

    def place(a, o):
        s = head[a, o]

        @pl.when(s < 0)
        def _():
            put(a, a + o, jnp.zeros((B, B), BF16))

        @pl.when(s >= 0)
        def _():
            rest = after[a, jnp.maximum(s, 0)]

            @pl.when(rest < 0)
            def _():
                put(a, a + o, scaled(a, s).astype(BF16))

            @pl.when(rest >= 0)
            def _():
                acc[...] = scaled(a, s)

                def more(t):
                    acc[...] = acc[...] + scaled(a, t)
                    return after[a, t]

                lax.while_loop(lambda t: t >= 0, more, rest)
                put(a, a + o, acc[...].astype(BF16))

    edge[rows(0), rows(1)] = jnp.zeros((B, B), BF16)
    edge[rows(3), rows(2)] = jnp.zeros((B, B), BF16)
    for a in range(ROWS):
        copies[a].wait()
        for o in range(SPAN):
            place(a, o)
    terms = dot(turned, edge[...]).T.astype(BF16)
    to_right[pl.ds(HANDED, 2 * B), :] = terms[: 2 * B]
    to_left[pl.ds(HANDED, 2 * B), :] = terms[2 * B :]


def first_local_kernel(own, edge, onsite, y0, diag, sym, edge_t, base):
    for a in range(ROWS):
        for b in range(a + 1):
            value = own[rows(a), rows(b)].astype(F32) + flip(own[rows(b), rows(a)])
            sym[rows(a), rows(b)] = value.astype(BF16)
            if b < a:
                sym[rows(b), rows(a)] = value.T.astype(BF16)
    for a in range(ROWS):
        for j in range(4):
            edge_t[rows(j), rows(a)] = flip(edge[rows(a), rows(j)]).astype(BF16)
    diag[...] = ALPHA * (onsite[...] - SHIFT)
    base[...] = diag[...] * y0[...].astype(F32) + dot(sym[...], y0[...])


def forward(a, base, edge, right, left):
    wide = 1 if a == 0 else 2
    skip = 1 if a == ROWS - 1 else 0
    total = base[rows(a), :] + dot(edge[rows(a), rows(0, wide)], right(0, wide))
    return total + dot(edge[rows(a), rows(2 + skip, 2 - skip)], left(skip, 2 - skip))


def terms_of(a, got_left, got_right, start):
    got = got_left if a < 2 else got_right
    return got[pl.ds(start + (a % 2) * B, B), :].astype(F32)


def send_parts(edge_t, y, send_right, send_left):
    send_right[pl.ds(0, 2 * B), :] = y[pl.ds(2 * B, 2 * B), :]
    send_left[pl.ds(0, 2 * B), :] = y[pl.ds(0, 2 * B), :]
    send_right[pl.ds(2 * B, B), :] = dot(edge_t[rows(0), :], y[...]).astype(BF16)
    send_right[pl.ds(3 * B, B), :] = dot(edge_t[rows(1), rows(1, 3)], y[rows(1, 3), :]).astype(BF16)
    send_left[pl.ds(2 * B, B), :] = dot(edge_t[rows(2), rows(0, 3)], y[rows(0, 3), :]).astype(BF16)
    send_left[pl.ds(3 * B, B), :] = dot(edge_t[rows(3), :], y[...]).astype(BF16)


def first_post_kernel(base, edge_in, edge_t_in, to_right, to_left, got_left, got_right, edge, edge_t, y, send_right, send_left):
    edge[...] = edge_in[...]
    edge_t[...] = edge_t_in[...]
    for i, (r, c) in enumerate(TO_LEFT):
        block = read_block(got_right, i).astype(F32)
        edge_t[rows(r), rows(c)] = (edge_t[rows(r), rows(c)].astype(F32) + block).astype(BF16)
        edge[rows(c), rows(r)] = (edge[rows(c), rows(r)].astype(F32) + block.T).astype(BF16)
    for i, (c, p) in enumerate(TO_RIGHT):
        block = read_block(got_left, i).astype(F32)
        r = p - 8
        edge_t[rows(c), rows(r)] = (edge_t[rows(c), rows(r)].astype(F32) + block).astype(BF16)
        edge[rows(r), rows(c)] = (edge[rows(r), rows(c)].astype(F32) + block.T).astype(BF16)
    halo = HANDED + 2 * B

    def right(i, n):
        return got_right[pl.ds(halo + i * B, n * B), :]

    def left(i, n):
        return got_left[pl.ds(halo + (2 + i) * B, n * B), :]

    for a in range(ROWS):
        total = forward(a, base, edge, right, left) + terms_of(a, got_left, got_right, HANDED)
        for places, source, got, start in ((TO_LEFT, to_left, got_left, 0), (TO_RIGHT, to_right, got_right, 8)):
            for i, (row, p) in enumerate(places):
                if row == a:
                    total += dot(read_block(source, i), got[pl.ds(halo + (p - start) * B, B), :])
        y[rows(a), :] = (0.5 * total).astype(BF16)
    send_parts(edge_t, y, send_right, send_left)


def receive(base, edge, got_left, got_right, y):
    def right(i, n):
        return got_right[rows(i, n), :]

    def left(i, n):
        return got_left[rows(i, n), :]

    for a in range(ROWS):
        total = forward(a, base, edge, right, left) + terms_of(a, got_left, got_right, 2 * B)
        y[rows(a), :] = total.astype(BF16)


def post_kernel(base, edge, edge_t, got_left, got_right, y, send_right, send_left):
    receive(base, edge, got_left, got_right, y)
    send_parts(edge_t, y, send_right, send_left)


def last_kernel(base, edge, got_left, got_right, y, gram):
    receive(base, edge, got_left, got_right, y)
    gram[...] = lax.dot_general(y[...], y[...], (((0,), (0,)), ((), ())), preferred_element_type=F32)


def local_kernel(sym, diag, y, older, base):
    base[...] = diag[...] * y[...].astype(F32) - older[...].astype(F32) + dot(sym[...], y[...])


def lane_fill(x, c):
    return jnp.take_along_axis(x, jnp.full((T, K), c, jnp.int32), axis=1)


def row_fill(x, j):
    return jnp.take_along_axis(x, jnp.full((T, K), j, jnp.int32), axis=0)


def inverse_factor(gram, inverse):
    count = K // T
    lane = lax.broadcasted_iota(jnp.int32, (T, K), 1)
    sub = lax.broadcasted_iota(jnp.int32, (T, K), 0)
    tiles = [gram[pl.ds(T * t, T), :] for t in range(count)]
    for k in range(count):
        first = T * k
        inside = (lane >= first) & (lane < first + T)
        spread = [lane_fill(tiles[k], first + c) for c in range(T)]
        rest = jnp.where(inside, 0.0, tiles[k])
        steps = []
        scale = jnp.zeros((T, K), F32)
        for j in range(T):
            pivot = row_fill(spread[j], j)
            inv = 1.0 / pivot
            ratios = {c: row_fill(spread[c], j) * inv for c in range(j + 1, T)}
            row = jnp.where(lane == first + j, 1.0, row_fill(rest, j)) * inv
            steps.append((ratios, row))
            rest = rest - jnp.where(sub > j, spread[j], 0.0) * row
            for c in range(j + 1, T):
                spread[c] = spread[c] - spread[j] * ratios[c]
            scale = jnp.where(sub == j, lax.rsqrt(pivot), scale)
        unit = jnp.where(lane < first + sub, rest, jnp.where(lane == first + sub, 1.0, 0.0))
        inverse[pl.ds(first, T), :] = unit * scale
        for t in range(k + 1, count):
            factors = [lane_fill(tiles[t], first + c) for c in range(T)]
            value = jnp.where(inside, 0.0, tiles[t])
            for j, (ratios, row) in enumerate(steps):
                value = value - factors[j] * row
                for c in range(j + 1, T):
                    factors[c] = factors[c] - factors[j] * ratios[c]
            tiles[t] = value


def finish_kernel(scale, gram, y, basis, inverse):
    inverse_factor(gram, inverse)
    value = inverse[...] * scale
    high = value.astype(BF16)
    low = (value - high.astype(F32)).astype(BF16)
    dims = (((1,), (1,)), ((), ()))
    basis[...] = lax.dot_general(y[...], high, dims, preferred_element_type=F32) + lax.dot_general(
        y[...], low, dims, preferred_element_type=F32
    )


VMEM = pl.BlockSpec(memory_space=pltpu.VMEM)
SMEM = pl.BlockSpec(memory_space=pltpu.SMEM)
HBM = pl.BlockSpec(memory_space=pltpu.HBM)
LIMIT = 20 * 1024 * 1024


def call(kernel, outs, specs, flops, size, scratch=(), aliases=None):
    return pl.pallas_call(
        kernel,
        out_shape=[jax.ShapeDtypeStruct(*out) for out in outs],
        in_specs=list(specs),
        out_specs=[VMEM] * len(outs),
        scratch_shapes=list(scratch),
        input_output_aliases=aliases or {},
        cost_estimate=pl.CostEstimate(flops=flops, bytes_accessed=size, transcendentals=0),
        compiler_params=pltpu.CompilerParams(vmem_limit_bytes=LIMIT),
    )


def ring(value, step):
    count = lax.axis_size(AXES)
    return lax.ppermute(value, AXES, [(i, (i + step) % count) for i in range(count)])


def group_sum(value, stride, size):
    count = lax.axis_size(AXES)
    parts = [value]
    for step in range(1, size):
        pairs = []
        for i in range(count):
            digit = (i // stride) % size
            partner = digit ^ step if size & (size - 1) == 0 else (digit + step) % size
            pairs.append((i, i + (partner - digit) * stride))
        parts.append(lax.ppermute(value, AXES, pairs))
    return sum(parts[1:], parts[0])


def digits():
    out, stride = [], 1
    for axis, cut in (("col", 4), ("row", 2)):
        left = lax.axis_size(axis)
        while left > 1:
            size = cut if left % cut == 0 else left
            out.append((stride, size))
            stride *= size
            left //= size
            cut = left if axis == "row" else cut
    return out


def local(blocks, block_scales, columns, live, onsite, start_vectors):
    slots = columns.shape[1]
    total = ROWS * lax.axis_size(AXES)
    column = ((OWN, 1), F32)
    tall = ((OWN, K), BF16)
    tall32 = ((OWN, K), F32)
    square = ((OWN, OWN), BF16)
    message = ((HANDED + 2 * B + OWN, K), BF16)
    product = 2 * OWN * OWN * K

    y0 = start_vectors
    own, edge, to_right, to_left = call(
        functools.partial(prep_kernel, total),
        [square, square, message, message],
        [SMEM, SMEM, SMEM, HBM, VMEM],
        product,
        10_000_000,
        [
            pltpu.VMEM((ROWS, slots, B, B), BF16),
            pltpu.VMEM((B, B), F32),
            pltpu.SMEM((ROWS, SPAN), jnp.int32),
            pltpu.SMEM((ROWS, slots), jnp.int32),
            pltpu.SemaphoreType.DMA((ROWS,)),
        ],
    )(block_scales, columns, live, blocks, y0)
    got_left, got_right = ring(to_right, 1), ring(to_left, -1)
    diag, sym, edge_t, base = call(first_local_kernel, [column, square, square, tall32], [VMEM] * 4, product, 10_000_000)(
        own, edge, onsite[:, None], y0
    )
    edge, edge_t, y, send_right, send_left = call(
        first_post_kernel, [square, square, tall, tall, tall], [VMEM] * 7, 2 * product, 9_000_000, (), {1: 0, 2: 1}
    )(base, edge, edge_t, to_right, to_left, got_left, got_right)
    older = y0
    for step in range(1, DEG):
        got_left, got_right = ring(send_right, 1), ring(send_left, -1)
        base = call(local_kernel, [tall32], [VMEM] * 4, product, 3_500_000)(sym, diag, y, older)[0]
        older = y
        if step < DEG - 1:
            y, send_right, send_left = call(post_kernel, [tall, tall, tall], [VMEM] * 5, 2 * product, 6_000_000)(
                base, edge, edge_t, got_left, got_right
            )
        else:
            y, gram = call(last_kernel, [tall, ((K, K), F32)], [VMEM] * 4, product, 4_000_000)(
                base, edge, got_left, got_right
            )
    for stride, size in digits():
        gram = group_sum(gram, stride, size)
    scale = float(np.sqrt(total * B))
    return call(
        functools.partial(finish_kernel, scale), [tall32], [VMEM] * 2, 2 * product, 1_000_000, [pltpu.VMEM((K, K), F32)]
    )(gram, y)[0]


def solution(mesh):
    return jax.shard_map(
        local,
        mesh=mesh,
        in_specs=(
            P(AXES, None, None, None),
            P(AXES, None),
            P(AXES, None),
            P(AXES),
            P(AXES),
            P(AXES, None),
        ),
        out_specs=P(AXES, None),
        check_vma=False,
    )
```

```python
import functools

import jax
import jax.numpy as jnp
import numpy as np
from jax import lax
from jax.experimental import pallas as pl
from jax.experimental.pallas import tpu as pltpu
from jax.sharding import PartitionSpec as P

DEG = 5
B = 256
K = 128
ROWS = 4
OWN = ROWS * B
REACH = 4
SPAN = 2 * REACH + 1
AXES = ("row", "col")
ALPHA = 2.0 / 1.1
SHIFT = 0.2
F32 = jnp.float32
BF16 = jnp.bfloat16
EDGE = (8, 9, 2, 3)
TO_RIGHT = ((2, 10), (3, 10), (3, 11))
TO_LEFT = ((0, 0), (0, 1), (1, 1))
HANDED = 3 * 2 * B
T = 8


def rows(i, n=1):
    return pl.ds(i * B, n * B)


def dot(a, b):
    return jnp.dot(a, b, preferred_element_type=F32)


def read_block(ref, i):
    return jnp.concatenate([ref[rows(2 * i), :], ref[rows(2 * i + 1), :]], axis=1)


def flip(block):
    return block.astype(F32).T


def prep_kernel(total, scales, columns, live, blocks, y0, own, edge, to_e, to_o, buf, acc, head, after, sem):
    copies = [pltpu.make_async_copy(blocks.at[a], buf.at[a], sem.at[a]) for a in range(ROWS)]
    for copy in copies:
        copy.start()
    first = lax.axis_index(AXES) * ROWS
    for a in range(ROWS):
        for o in range(SPAN):
            head[a, o] = -1

        def chain(s, carry, a=a):
            o = lax.rem(columns[a, s] - (first + a) + REACH + total, total)
            after[a, s] = head[a, o]
            head[a, o] = s
            return carry

        lax.fori_loop(0, live[a], chain, 0)
    turned = flip(y0[...]).astype(BF16)
    for target in (to_e, to_o):
        target[pl.ds(HANDED + 2 * B, OWN), :] = y0[...]
    even = lax.rem(lax.axis_index(AXES), 2) == 0

    def put_message(right, start, value):
        for case, target in ((even, to_e if right else to_o), (~even, to_o if right else to_e)):

            @pl.when(case)
            def _(target=target):
                target[pl.ds(start, value.shape[0]), :] = value

    def put(a, p, value):
        if 4 <= p < 8:
            own[rows(a), rows(p - 4)] = value
        elif p in EDGE:
            edge[rows(a), rows(EDGE.index(p))] = value
        else:
            right = p > 8
            i = (TO_RIGHT if right else TO_LEFT).index((a, p))
            put_message(right, 2 * i * B, value[:, :K])
            put_message(right, (2 * i + 1) * B, value[:, K:])

    def scaled(a, s):
        return (scales[a, s] * ALPHA) * buf[a, s].astype(F32)

    def place(a, o):
        s = head[a, o]

        @pl.when(s < 0)
        def _():
            put(a, a + o, jnp.zeros((B, B), BF16))

        @pl.when(s >= 0)
        def _():
            rest = after[a, jnp.maximum(s, 0)]

            @pl.when(rest < 0)
            def _():
                put(a, a + o, scaled(a, s).astype(BF16))

            @pl.when(rest >= 0)
            def _():
                acc[...] = scaled(a, s)

                def more(t):
                    acc[...] = acc[...] + scaled(a, t)
                    return after[a, t]

                lax.while_loop(lambda t: t >= 0, more, rest)
                put(a, a + o, acc[...].astype(BF16))

    edge[rows(0), rows(1)] = jnp.zeros((B, B), BF16)
    edge[rows(3), rows(2)] = jnp.zeros((B, B), BF16)
    for a in range(ROWS):
        copies[a].wait()
        for o in range(SPAN):
            place(a, o)
    terms = dot(turned, edge[...]).T.astype(BF16)
    put_message(True, HANDED, terms[: 2 * B])
    put_message(False, HANDED, terms[2 * B :])


def first_local_kernel(own, edge, onsite, y0, diag, sym, edge_t, base):
    for a in range(ROWS):
        for b in range(a + 1):
            value = own[rows(a), rows(b)].astype(F32) + flip(own[rows(b), rows(a)])
            sym[rows(a), rows(b)] = value.astype(BF16)
            if b < a:
                sym[rows(b), rows(a)] = value.T.astype(BF16)
    for a in range(ROWS):
        for j in range(4):
            edge_t[rows(j), rows(a)] = flip(edge[rows(a), rows(j)]).astype(BF16)
    diag[...] = ALPHA * (onsite[...] - SHIFT)
    base[...] = diag[...] * y0[...].astype(F32) + dot(sym[...], y0[...])


def by_parity(body):
    parity = lax.rem(lax.axis_index(AXES), 2)
    for value in (0, 1):

        @pl.when(parity == value)
        def _(even=value == 0):
            body(even)


def halo_right(a, edge, got, halo=0):
    wide = 1 if a == 0 else 2
    return dot(edge[rows(a), rows(0, wide)], got[pl.ds(halo, wide * B), :])


def halo_left(a, edge, got, halo=0):
    skip = 1 if a == ROWS - 1 else 0
    return dot(edge[rows(a), rows(2 + skip, 2 - skip)], got[pl.ds(halo + skip * B, (2 - skip) * B), :])


def terms_of(a, got_left, got_right, start=0):
    got = got_left if a < 2 else got_right
    return got[pl.ds(start + (a % 2) * B, B), :].astype(F32)


HALF = K // 2


def half_mask(half):
    lane = lax.broadcasted_iota(jnp.int32, (B, K), 1)
    return (lane < HALF) if half == 0 else (lane >= HALF)


def pack(half, edge_t, y, send_right, send_left, spare):
    mine = half_mask(half)
    for a in range(ROWS):
        value = jnp.where(mine, y[rows(a), :].astype(F32), 0.0)
        spare[rows(a), :] = pltpu.roll(value, HALF, 1).astype(BF16)

    def put(target, i, row, terms):
        target[rows(i), :] = jnp.where(mine, y[rows(row), :].astype(F32), terms).astype(BF16)

    put(send_right, 0, 2, dot(edge_t[rows(0), :], spare[...]))
    put(send_right, 1, 3, dot(edge_t[rows(1), rows(1, 3)], spare[rows(1, 3), :]))
    put(send_left, 0, 0, dot(edge_t[rows(2), rows(0, 3)], spare[rows(0, 3), :]))
    put(send_left, 1, 1, dot(edge_t[rows(3), :], spare[...]))


def first_post_kernel(base, edge_in, edge_t_in, to_e, to_o, got_e, got_o, edge, edge_t, y, send_e, send_o, send_e2, send_o2, spare):
    edge[...] = edge_in[...]
    edge_t[...] = edge_t_in[...]

    def body(even):
        to_right, to_left = (to_e, to_o) if even else (to_o, to_e)
        got_right, got_left = (got_e, got_o) if even else (got_o, got_e)
        for i, (r, c) in enumerate(TO_LEFT):
            block = read_block(got_right, i).astype(F32)
            edge_t[rows(r), rows(c)] = (edge_t[rows(r), rows(c)].astype(F32) + block).astype(BF16)
            edge[rows(c), rows(r)] = (edge[rows(c), rows(r)].astype(F32) + block.T).astype(BF16)
        for i, (c, p) in enumerate(TO_RIGHT):
            block = read_block(got_left, i).astype(F32)
            r = p - 8
            edge_t[rows(c), rows(r)] = (edge_t[rows(c), rows(r)].astype(F32) + block).astype(BF16)
            edge[rows(r), rows(c)] = (edge[rows(r), rows(c)].astype(F32) + block.T).astype(BF16)
        halo = HANDED + 2 * B
        for a in range(ROWS):
            total = base[rows(a), :] + halo_right(a, edge, got_right, halo)
            total += halo_left(a, edge, got_left, halo + 2 * B) + terms_of(a, got_left, got_right, HANDED)
            for places, source, got, start in ((TO_LEFT, to_left, got_left, 0), (TO_RIGHT, to_right, got_right, 8)):
                for i, (row, p) in enumerate(places):
                    if row == a:
                        total += dot(read_block(source, i), got[pl.ds(halo + (p - start) * B, B), :])
            y[rows(a), :] = (0.5 * total).astype(BF16)
        pack(0, edge_t, y, *((send_e, send_o) if even else (send_o, send_e)), spare)
        pack(1, edge_t, y, *((send_e2, send_o2) if even else (send_o2, send_e2)), spare)

    by_parity(body)


def local_kernel(sym, diag, y, older, base):
    base[...] = diag[...] * y[...].astype(F32) - older[...].astype(F32) + dot(sym[...], y[...])


def receive(even, half, base, edge, got_e, got_o, y_in, y):
    got_right, got_left = (got_e, got_o) if even else (got_o, got_e)
    for a in range(ROWS):
        total = base[rows(a), :] + halo_right(a, edge, got_right) + halo_left(a, edge, got_left)
        total += pltpu.roll(terms_of(a, got_left, got_right), HALF, 1)
        y[rows(a), :] = jnp.where(half_mask(half), total, y_in[rows(a), :].astype(F32)).astype(BF16)


def post_kernel(half, base, edge, edge_t, got_e, got_o, y_in, y, send_e, send_o, spare):
    def body(even):
        receive(even, half, base, edge, got_e, got_o, y_in, y)
        pack(half, edge_t, y, *((send_e, send_o) if even else (send_o, send_e)), spare)

    by_parity(body)


def last_first_kernel(base, edge, got_e, got_o, y_in, y):
    by_parity(lambda even: receive(even, 0, base, edge, got_e, got_o, y_in, y))


def last_kernel(base, edge, got_e, got_o, y_in, y, gram):
    by_parity(lambda even: receive(even, 1, base, edge, got_e, got_o, y_in, y))
    gram[...] = lax.dot_general(y[...], y[...], (((0,), (0,)), ((), ())), preferred_element_type=F32)


def lane_fill(x, c):
    return jnp.take_along_axis(x, jnp.full((T, K), c, jnp.int32), axis=1)


def row_fill(x, j):
    return jnp.take_along_axis(x, jnp.full((T, K), j, jnp.int32), axis=0)


def inverse_factor(gram, inverse):
    count = K // T
    lane = lax.broadcasted_iota(jnp.int32, (T, K), 1)
    sub = lax.broadcasted_iota(jnp.int32, (T, K), 0)
    tiles = [gram[pl.ds(T * t, T), :] for t in range(count)]
    for k in range(count):
        first = T * k
        inside = (lane >= first) & (lane < first + T)
        spread = [lane_fill(tiles[k], first + c) for c in range(T)]
        rest = jnp.where(inside, 0.0, tiles[k])
        steps = []
        scale = jnp.zeros((T, K), F32)
        for j in range(T):
            pivot = row_fill(spread[j], j)
            inv = 1.0 / pivot
            ratios = {c: row_fill(spread[c], j) * inv for c in range(j + 1, T)}
            row = jnp.where(lane == first + j, 1.0, row_fill(rest, j)) * inv
            steps.append((ratios, row))
            rest = rest - jnp.where(sub > j, spread[j], 0.0) * row
            for c in range(j + 1, T):
                spread[c] = spread[c] - spread[j] * ratios[c]
            scale = jnp.where(sub == j, lax.rsqrt(pivot), scale)
        unit = jnp.where(lane < first + sub, rest, jnp.where(lane == first + sub, 1.0, 0.0))
        inverse[pl.ds(first, T), :] = unit * scale
        for t in range(k + 1, count):
            factors = [lane_fill(tiles[t], first + c) for c in range(T)]
            value = jnp.where(inside, 0.0, tiles[t])
            for j, (ratios, row) in enumerate(steps):
                value = value - factors[j] * row
                for c in range(j + 1, T):
                    factors[c] = factors[c] - factors[j] * ratios[c]
            tiles[t] = value


def finish_kernel(scale, gram, y, basis, inverse):
    inverse_factor(gram, inverse)
    value = inverse[...] * scale
    high = value.astype(BF16)
    low = (value - high.astype(F32)).astype(BF16)
    dims = (((1,), (1,)), ((), ()))
    basis[...] = lax.dot_general(y[...], high, dims, preferred_element_type=F32) + lax.dot_general(
        y[...], low, dims, preferred_element_type=F32
    )


VMEM = pl.BlockSpec(memory_space=pltpu.VMEM)
SMEM = pl.BlockSpec(memory_space=pltpu.SMEM)
HBM = pl.BlockSpec(memory_space=pltpu.HBM)
LIMIT = 20 * 1024 * 1024
PREP_LIMIT = 57 * 1000 * 1000


def call(kernel, outs, specs, flops, size, scratch=(), aliases=None, limit=LIMIT):
    return pl.pallas_call(
        kernel,
        out_shape=[jax.ShapeDtypeStruct(*out) for out in outs],
        in_specs=list(specs),
        out_specs=[VMEM] * len(outs),
        scratch_shapes=list(scratch),
        input_output_aliases=aliases or {},
        cost_estimate=pl.CostEstimate(flops=flops, bytes_accessed=size, transcendentals=0),
        compiler_params=pltpu.CompilerParams(vmem_limit_bytes=limit),
    )


def swap_o(value):
    count = lax.axis_size(AXES)
    return lax.ppermute(value, AXES, [(i, (i + 1 if i % 2 else i - 1) % count) for i in range(count)])


def swap_e(value):
    return lax.ppermute(value, AXES, [(i, i ^ 1) for i in range(lax.axis_size(AXES))])


def exchange(send_e, send_o):
    got_o = swap_o(send_o)
    return swap_e(send_e), got_o


def group_sum(value, stride, size):
    count = lax.axis_size(AXES)
    parts = [value]
    for step in range(1, size):
        pairs = []
        for i in range(count):
            digit = (i // stride) % size
            partner = digit ^ step if size & (size - 1) == 0 else (digit + step) % size
            pairs.append((i, i + (partner - digit) * stride))
        parts.append(lax.ppermute(value, AXES, pairs))
    return sum(parts[1:], parts[0])


def digits():
    out, stride = [], 1
    for axis, cut in (("col", 4), ("row", 2)):
        left = lax.axis_size(axis)
        while left > 1:
            size = cut if left % cut == 0 else left
            out.append((stride, size))
            stride *= size
            left //= size
            cut = left if axis == "row" else cut
    return out


def local(blocks, block_scales, columns, live, onsite, start_vectors):
    slots = columns.shape[1]
    total = ROWS * lax.axis_size(AXES)
    column = ((OWN, 1), F32)
    tall = ((OWN, K), BF16)
    tall32 = ((OWN, K), F32)
    square = ((OWN, OWN), BF16)
    message = ((HANDED + 2 * B + OWN, K), BF16)
    product = 2 * OWN * OWN * K

    y0 = start_vectors
    own, edge, to_e, to_o = call(
        functools.partial(prep_kernel, total),
        [square, square, message, message],
        [SMEM, SMEM, SMEM, HBM, VMEM],
        product,
        10_000_000,
        [
            pltpu.VMEM((ROWS, slots, B, B), BF16),
            pltpu.VMEM((B, B), F32),
            pltpu.SMEM((ROWS, SPAN), jnp.int32),
            pltpu.SMEM((ROWS, slots), jnp.int32),
            pltpu.SemaphoreType.DMA((ROWS,)),
        ],
        limit=PREP_LIMIT,
    )(block_scales, columns, live, blocks, y0)
    got_o, got_e = swap_o(to_o), swap_e(to_e)
    diag, sym, edge_t, base = call(first_local_kernel, [column, square, square, tall32], [VMEM] * 4, product, 10_000_000)(
        own, edge, onsite[:, None], y0
    )
    part = ((2 * B, K), BF16)
    spare = [pltpu.VMEM((OWN, K), BF16)]
    edge, edge_t, y, *sends = call(
        first_post_kernel, [square, square, tall, part, part, part, part], [VMEM] * 7, 3 * product, 9_000_000, spare, {1: 0, 2: 1}
    )(base, edge, edge_t, to_e, to_o, got_e, got_o)
    older = y0
    got = exchange(*sends[:2])
    got2 = exchange(*sends[2:])
    for step in range(1, DEG):
        base = call(local_kernel, [tall32], [VMEM] * 4, product, 3_500_000)(sym, diag, y, older)[0]
        older = y
        if step < DEG - 1:
            outs = [tall, part, part]
            specs = [VMEM] * 6
            y, *sends = call(functools.partial(post_kernel, 0), outs, specs, 2 * product, 6_000_000, spare)(
                base, edge, edge_t, *got, y
            )
            got = exchange(*sends)
            y, *sends = call(functools.partial(post_kernel, 1), outs, specs, 2 * product, 6_000_000, spare)(
                base, edge, edge_t, *got2, y
            )
            got2 = exchange(*sends)
        else:
            y = call(last_first_kernel, [tall], [VMEM] * 5, product, 4_000_000)(base, edge, *got, y)[0]
            y, gram = call(last_kernel, [tall, ((K, K), F32)], [VMEM] * 5, product, 4_000_000)(base, edge, *got2, y)
    for stride, size in digits():
        gram = group_sum(gram, stride, size)
    scale = float(np.sqrt(total * B))
    return call(
        functools.partial(finish_kernel, scale), [tall32], [VMEM] * 2, 2 * product, 1_000_000, [pltpu.VMEM((K, K), F32)]
    )(gram, y)[0]


def solution(mesh):
    return jax.shard_map(
        local,
        mesh=mesh,
        in_specs=(
            P(AXES, None, None, None),
            P(AXES, None),
            P(AXES, None),
            P(AXES),
            P(AXES),
            P(AXES, None),
        ),
        out_specs=P(AXES, None),
        check_vma=False,
    )
```

```python
import functools

import jax
import jax.numpy as jnp
import numpy as np
from jax import lax
from jax.experimental import pallas as pl
from jax.experimental.pallas import tpu as pltpu
from jax.sharding import PartitionSpec as P

DEG = 5
B = 256
K = 128
ROWS = 4
OWN = ROWS * B
REACH = 4
SPAN = 2 * REACH + 1
AXES = ("row", "col")
ALPHA = 2.0 / 1.1
SHIFT = 0.2
F32 = jnp.float32
BF16 = jnp.bfloat16
EDGE = (8, 9, 2, 3)
TO_RIGHT = ((2, 10), (3, 10), (3, 11))
TO_LEFT = ((0, 0), (0, 1), (1, 1))
HANDED = 3 * 2 * B
T = 8


def rows(i, n=1):
    return pl.ds(i * B, n * B)


def dot(a, b):
    return jnp.dot(a, b, preferred_element_type=F32)


def read_block(ref, i):
    return jnp.concatenate([ref[rows(2 * i), :], ref[rows(2 * i + 1), :]], axis=1)


def flip(block):
    return block.astype(F32).T


def prep_kernel(total, scales, columns, live, blocks, y0, own, edge, to_e, to_o, buf, acc, head, after, sem):
    copies = [pltpu.make_async_copy(blocks.at[a], buf.at[a], sem.at[a]) for a in range(ROWS)]
    for copy in copies:
        copy.start()
    first = lax.axis_index(AXES) * ROWS
    for a in range(ROWS):
        for o in range(SPAN):
            head[a, o] = -1

        def chain(s, carry, a=a):
            o = lax.rem(columns[a, s] - (first + a) + REACH + total, total)
            after[a, s] = head[a, o]
            head[a, o] = s
            return carry

        lax.fori_loop(0, live[a], chain, 0)
    turned = flip(y0[...]).astype(BF16)
    for target in (to_e, to_o):
        target[pl.ds(HANDED + 2 * B, OWN), :] = y0[...]
    even = lax.rem(lax.axis_index(AXES), 2) == 0

    def put_message(right, start, value):
        for case, target in ((even, to_e if right else to_o), (~even, to_o if right else to_e)):

            @pl.when(case)
            def _(target=target):
                target[pl.ds(start, value.shape[0]), :] = value

    def put(a, p, value):
        if 4 <= p < 8:
            own[rows(a), rows(p - 4)] = value
        elif p in EDGE:
            edge[rows(a), rows(EDGE.index(p))] = value
        else:
            right = p > 8
            i = (TO_RIGHT if right else TO_LEFT).index((a, p))
            put_message(right, 2 * i * B, value[:, :K])
            put_message(right, (2 * i + 1) * B, value[:, K:])

    def scaled(a, s):
        return (scales[a, s] * ALPHA) * buf[a, s].astype(F32)

    def place(a, o):
        s = head[a, o]

        @pl.when(s < 0)
        def _():
            put(a, a + o, jnp.zeros((B, B), BF16))

        @pl.when(s >= 0)
        def _():
            rest = after[a, jnp.maximum(s, 0)]

            @pl.when(rest < 0)
            def _():
                put(a, a + o, scaled(a, s).astype(BF16))

            @pl.when(rest >= 0)
            def _():
                acc[...] = scaled(a, s)

                def more(t):
                    acc[...] = acc[...] + scaled(a, t)
                    return after[a, t]

                lax.while_loop(lambda t: t >= 0, more, rest)
                put(a, a + o, acc[...].astype(BF16))

    edge[rows(0), rows(1)] = jnp.zeros((B, B), BF16)
    edge[rows(3), rows(2)] = jnp.zeros((B, B), BF16)
    for a in range(ROWS):
        copies[a].wait()
        for o in range(SPAN):
            place(a, o)
    terms = dot(turned, edge[...]).T.astype(BF16)
    put_message(True, HANDED, terms[: 2 * B])
    put_message(False, HANDED, terms[2 * B :])


def first_local_kernel(own, edge, onsite, y0, diag, sym, edge_t, base):
    for a in range(ROWS):
        for b in range(a + 1):
            value = own[rows(a), rows(b)].astype(F32) + flip(own[rows(b), rows(a)])
            sym[rows(a), rows(b)] = value.astype(BF16)
            if b < a:
                sym[rows(b), rows(a)] = value.T.astype(BF16)
    for a in range(ROWS):
        for j in range(4):
            edge_t[rows(j), rows(a)] = flip(edge[rows(a), rows(j)]).astype(BF16)
    diag[...] = ALPHA * (onsite[...] - SHIFT)
    base[...] = diag[...] * y0[...].astype(F32) + dot(sym[...], y0[...])


def by_parity(body):
    parity = lax.rem(lax.axis_index(AXES), 2)
    for value in (0, 1):

        @pl.when(parity == value)
        def _(even=value == 0):
            body(even)


def halo_right(a, edge, got, halo=0):
    wide = 1 if a == 0 else 2
    return dot(edge[rows(a), rows(0, wide)], got[pl.ds(halo, wide * B), :])


def halo_left(a, edge, got, halo=0):
    skip = 1 if a == ROWS - 1 else 0
    return dot(edge[rows(a), rows(2 + skip, 2 - skip)], got[pl.ds(halo + skip * B, (2 - skip) * B), :])


def terms_of(a, got_left, got_right, start=0):
    got = got_left if a < 2 else got_right
    return got[pl.ds(start + (a % 2) * B, B), :].astype(F32)


HALF = K // 2


def half_mask(half):
    lane = lax.broadcasted_iota(jnp.int32, (B, K), 1)
    return (lane < HALF) if half == 0 else (lane >= HALF)


def pack(half, edge_t, y, send_right, send_left, spare):
    mine = half_mask(half)
    for a in range(ROWS):
        value = jnp.where(mine, y[rows(a), :].astype(F32), 0.0)
        spare[rows(a), :] = pltpu.roll(value, HALF, 1).astype(BF16)

    def put(target, i, row, terms):
        target[rows(i), :] = jnp.where(mine, y[rows(row), :].astype(F32), terms).astype(BF16)

    put(send_right, 0, 2, dot(edge_t[rows(0), :], spare[...]))
    put(send_right, 1, 3, dot(edge_t[rows(1), rows(1, 3)], spare[rows(1, 3), :]))
    put(send_left, 0, 0, dot(edge_t[rows(2), rows(0, 3)], spare[rows(0, 3), :]))
    put(send_left, 1, 1, dot(edge_t[rows(3), :], spare[...]))


def first_post_kernel(base, edge_in, edge_t_in, to_e, to_o, got_e, got_o, edge, edge_t, y, send_e, send_o, send_e2, send_o2, spare):
    edge[...] = edge_in[...]
    edge_t[...] = edge_t_in[...]

    def body(even):
        to_right, to_left = (to_e, to_o) if even else (to_o, to_e)
        got_right, got_left = (got_e, got_o) if even else (got_o, got_e)
        for i, (r, c) in enumerate(TO_LEFT):
            block = read_block(got_right, i).astype(F32)
            edge_t[rows(r), rows(c)] = (edge_t[rows(r), rows(c)].astype(F32) + block).astype(BF16)
            edge[rows(c), rows(r)] = (edge[rows(c), rows(r)].astype(F32) + block.T).astype(BF16)
        for i, (c, p) in enumerate(TO_RIGHT):
            block = read_block(got_left, i).astype(F32)
            r = p - 8
            edge_t[rows(c), rows(r)] = (edge_t[rows(c), rows(r)].astype(F32) + block).astype(BF16)
            edge[rows(r), rows(c)] = (edge[rows(r), rows(c)].astype(F32) + block.T).astype(BF16)
        halo = HANDED + 2 * B
        for a in range(ROWS):
            total = base[rows(a), :] + halo_right(a, edge, got_right, halo)
            total += halo_left(a, edge, got_left, halo + 2 * B) + terms_of(a, got_left, got_right, HANDED)
            for places, source, got, start in ((TO_LEFT, to_left, got_left, 0), (TO_RIGHT, to_right, got_right, 8)):
                for i, (row, p) in enumerate(places):
                    if row == a:
                        total += dot(read_block(source, i), got[pl.ds(halo + (p - start) * B, B), :])
            y[rows(a), :] = (0.5 * total).astype(BF16)
        pack(0, edge_t, y, *((send_e, send_o) if even else (send_o, send_e)), spare)
        pack(1, edge_t, y, *((send_e2, send_o2) if even else (send_o2, send_e2)), spare)

    by_parity(body)


def local_kernel(sym, diag, y, older, base):
    base[...] = diag[...] * y[...].astype(F32) - older[...].astype(F32) + dot(sym[...], y[...])


def receive(even, half, base, edge, got_e, got_o, y_in, y):
    got_right, got_left = (got_e, got_o) if even else (got_o, got_e)
    for a in range(ROWS):
        total = base[rows(a), :] + halo_right(a, edge, got_right) + halo_left(a, edge, got_left)
        total += pltpu.roll(terms_of(a, got_left, got_right), HALF, 1)
        y[rows(a), :] = jnp.where(half_mask(half), total, y_in[rows(a), :].astype(F32)).astype(BF16)


def post_kernel(half, base, edge, edge_t, got_e, got_o, y_in, y, send_e, send_o, spare):
    def body(even):
        receive(even, half, base, edge, got_e, got_o, y_in, y)
        pack(half, edge_t, y, *((send_e, send_o) if even else (send_o, send_e)), spare)

    by_parity(body)


def last_first_kernel(base, edge, got_e, got_o, y_in, y):
    by_parity(lambda even: receive(even, 0, base, edge, got_e, got_o, y_in, y))


def last_kernel(base, edge, got_e, got_o, y_in, y, gram):
    by_parity(lambda even: receive(even, 1, base, edge, got_e, got_o, y_in, y))
    gram[...] = lax.dot_general(y[...], y[...], (((0,), (0,)), ((), ())), preferred_element_type=F32)


def lane_fill(x, c):
    return jnp.take_along_axis(x, jnp.full((T, K), c, jnp.int32), axis=1)


def row_fill(x, j):
    return jnp.take_along_axis(x, jnp.full((T, K), j, jnp.int32), axis=0)


def inverse_factor(gram, inverse):
    count = K // T
    lane = lax.broadcasted_iota(jnp.int32, (T, K), 1)
    sub = lax.broadcasted_iota(jnp.int32, (T, K), 0)
    tiles = [gram[pl.ds(T * t, T), :] for t in range(count)]
    for k in range(count):
        first = T * k
        inside = (lane >= first) & (lane < first + T)
        spread = [lane_fill(tiles[k], first + c) for c in range(T)]
        rest = jnp.where(inside, 0.0, tiles[k])
        steps = []
        scale = jnp.zeros((T, K), F32)
        for j in range(T):
            pivot = row_fill(spread[j], j)
            inv = 1.0 / pivot
            ratios = {c: row_fill(spread[c], j) * inv for c in range(j + 1, T)}
            row = jnp.where(lane == first + j, 1.0, row_fill(rest, j)) * inv
            steps.append((ratios, row))
            rest = rest - jnp.where(sub > j, spread[j], 0.0) * row
            for c in range(j + 1, T):
                spread[c] = spread[c] - spread[j] * ratios[c]
            scale = jnp.where(sub == j, lax.rsqrt(pivot), scale)
        unit = jnp.where(lane < first + sub, rest, jnp.where(lane == first + sub, 1.0, 0.0))
        inverse[pl.ds(first, T), :] = unit * scale
        for t in range(k + 1, count):
            factors = [lane_fill(tiles[t], first + c) for c in range(T)]
            value = jnp.where(inside, 0.0, tiles[t])
            for j, (ratios, row) in enumerate(steps):
                value = value - factors[j] * row
                for c in range(j + 1, T):
                    factors[c] = factors[c] - factors[j] * ratios[c]
            tiles[t] = value


def finish_kernel(scale, gram, y, basis, inverse):
    inverse_factor(gram, inverse)
    value = inverse[...] * scale
    high = value.astype(BF16)
    low = (value - high.astype(F32)).astype(BF16)
    dims = (((1,), (1,)), ((), ()))
    basis[...] = lax.dot_general(y[...], high, dims, preferred_element_type=F32) + lax.dot_general(
        y[...], low, dims, preferred_element_type=F32
    )


VMEM = pl.BlockSpec(memory_space=pltpu.VMEM)
SMEM = pl.BlockSpec(memory_space=pltpu.SMEM)
HBM = pl.BlockSpec(memory_space=pltpu.HBM)
LIMIT = 20 * 1024 * 1024
PREP_LIMIT = LIMIT


def call(kernel, outs, specs, flops, size, scratch=(), aliases=None, limit=LIMIT):
    return pl.pallas_call(
        kernel,
        out_shape=[jax.ShapeDtypeStruct(*out) for out in outs],
        in_specs=list(specs),
        out_specs=[VMEM] * len(outs),
        scratch_shapes=list(scratch),
        input_output_aliases=aliases or {},
        cost_estimate=pl.CostEstimate(flops=flops, bytes_accessed=size, transcendentals=0),
        compiler_params=pltpu.CompilerParams(vmem_limit_bytes=limit),
    )


def swap_o(value):
    count = lax.axis_size(AXES)
    return lax.ppermute(value, AXES, [(i, (i + 1 if i % 2 else i - 1) % count) for i in range(count)])


def swap_e(value):
    return lax.ppermute(value, AXES, [(i, i ^ 1) for i in range(lax.axis_size(AXES))])


def exchange(send_e, send_o):
    got_o = swap_o(send_o)
    return swap_e(send_e), got_o


def group_sum(value, stride, size):
    count = lax.axis_size(AXES)
    parts = [value]
    for step in range(1, size):
        pairs = []
        for i in range(count):
            digit = (i // stride) % size
            partner = digit ^ step if size & (size - 1) == 0 else (digit + step) % size
            pairs.append((i, i + (partner - digit) * stride))
        parts.append(lax.ppermute(value, AXES, pairs))
    return sum(parts[1:], parts[0])


def digits():
    out, stride = [], 1
    for axis, cut in (("col", 4), ("row", 2)):
        left = lax.axis_size(axis)
        while left > 1:
            size = cut if left % cut == 0 else left
            out.append((stride, size))
            stride *= size
            left //= size
            cut = left if axis == "row" else cut
    return out


def local(blocks, block_scales, columns, live, onsite, start_vectors):
    slots = columns.shape[1]
    total = ROWS * lax.axis_size(AXES)
    column = ((OWN, 1), F32)
    tall = ((OWN, K), BF16)
    tall32 = ((OWN, K), F32)
    square = ((OWN, OWN), BF16)
    message = ((HANDED + 2 * B + OWN, K), BF16)
    product = 2 * OWN * OWN * K

    y0 = start_vectors
    own, edge, to_e, to_o = call(
        functools.partial(prep_kernel, total),
        [square, square, message, message],
        [SMEM, SMEM, SMEM, HBM, VMEM],
        product,
        10_000_000,
        [
            pltpu.VMEM((ROWS, slots, B, B), BF16),
            pltpu.VMEM((B, B), F32),
            pltpu.SMEM((ROWS, SPAN), jnp.int32),
            pltpu.SMEM((ROWS, slots), jnp.int32),
            pltpu.SemaphoreType.DMA((ROWS,)),
        ],
        limit=PREP_LIMIT,
    )(block_scales, columns, live, blocks, y0)
    got_o, got_e = swap_o(to_o), swap_e(to_e)
    diag, sym, edge_t, base = call(first_local_kernel, [column, square, square, tall32], [VMEM] * 4, product, 10_000_000)(
        own, edge, onsite[:, None], y0
    )
    part = ((2 * B, K), BF16)
    spare = [pltpu.VMEM((OWN, K), BF16)]
    edge, edge_t, y, *sends = call(
        first_post_kernel, [square, square, tall, part, part, part, part], [VMEM] * 7, 3 * product, 9_000_000, spare, {1: 0, 2: 1}
    )(base, edge, edge_t, to_e, to_o, got_e, got_o)
    older = y0
    got = exchange(*sends[:2])
    got2 = exchange(*sends[2:])
    for step in range(1, DEG):
        base = call(local_kernel, [tall32], [VMEM] * 4, product, 3_500_000)(sym, diag, y, older)[0]
        older = y
        if step < DEG - 1:
            outs = [tall, part, part]
            specs = [VMEM] * 6
            y, *sends = call(functools.partial(post_kernel, 0), outs, specs, 2 * product, 6_000_000, spare)(
                base, edge, edge_t, *got, y
            )
            got = exchange(*sends)
            y, *sends = call(functools.partial(post_kernel, 1), outs, specs, 2 * product, 6_000_000, spare)(
                base, edge, edge_t, *got2, y
            )
            got2 = exchange(*sends)
        else:
            y = call(last_first_kernel, [tall], [VMEM] * 5, product, 4_000_000)(base, edge, *got, y)[0]
            y, gram = call(last_kernel, [tall, ((K, K), F32)], [VMEM] * 5, product, 4_000_000)(base, edge, *got2, y)
    for stride, size in digits():
        gram = group_sum(gram, stride, size)
    scale = float(np.sqrt(total * B))
    return call(
        functools.partial(finish_kernel, scale), [tall32], [VMEM] * 2, 2 * product, 1_000_000, [pltpu.VMEM((K, K), F32)]
    )(gram, y)[0]


def solution(mesh):
    return jax.shard_map(
        local,
        mesh=mesh,
        in_specs=(
            P(AXES, None, None, None),
            P(AXES, None),
            P(AXES, None),
            P(AXES),
            P(AXES),
            P(AXES, None),
        ),
        out_specs=P(AXES, None),
        check_vma=False,
    )
```

```python
import functools

import jax
import jax.numpy as jnp
import numpy as np
from jax import lax
from jax.experimental import pallas as pl
from jax.experimental.pallas import tpu as pltpu
from jax.sharding import PartitionSpec as P

DEG = 5
B = 256
K = 128
ROWS = 4
OWN = ROWS * B
REACH = 4
SPAN = 2 * REACH + 1
AXES = ("row", "col")
ALPHA = 2.0 / 1.1
SHIFT = 0.2
F32 = jnp.float32
BF16 = jnp.bfloat16
EDGE = (8, 9, 2, 3)
TO_RIGHT = ((2, 10), (3, 10), (3, 11))
TO_LEFT = ((0, 0), (0, 1), (1, 1))
HANDED = 3 * 2 * B
T = 8


def rows(i, n=1):
    return pl.ds(i * B, n * B)


def dot(a, b):
    return jnp.dot(a, b, preferred_element_type=F32)


def read_block(ref, i):
    return jnp.concatenate([ref[rows(2 * i), :], ref[rows(2 * i + 1), :]], axis=1)


def flip(block):
    return block.astype(F32).T


def prep_kernel(total, scales, columns, live, blocks, y0, own, edge, to_e, to_o, buf, acc, head, after, sem):
    copies = [pltpu.make_async_copy(blocks.at[a], buf.at[a], sem.at[a]) for a in range(ROWS)]
    for copy in copies:
        copy.start()
    first = lax.axis_index(AXES) * ROWS
    for a in range(ROWS):
        for o in range(SPAN):
            head[a, o] = -1

        def chain(s, carry, a=a):
            o = lax.rem(columns[a, s] - (first + a) + REACH + total, total)
            after[a, s] = head[a, o]
            head[a, o] = s
            return carry

        lax.fori_loop(0, live[a], chain, 0)
    turned = flip(y0[...]).astype(BF16)
    for target in (to_e, to_o):
        target[pl.ds(HANDED + 2 * B, OWN), :] = y0[...]
    even = lax.rem(lax.axis_index(AXES), 2) == 0

    def put_message(right, start, value):
        for case, target in ((even, to_e if right else to_o), (~even, to_o if right else to_e)):

            @pl.when(case)
            def _(target=target):
                target[pl.ds(start, value.shape[0]), :] = value

    def put(a, p, value):
        if 4 <= p < 8:
            own[rows(a), rows(p - 4)] = value
        elif p in EDGE:
            edge[rows(a), rows(EDGE.index(p))] = value
        else:
            right = p > 8
            i = (TO_RIGHT if right else TO_LEFT).index((a, p))
            put_message(right, 2 * i * B, value[:, :K])
            put_message(right, (2 * i + 1) * B, value[:, K:])

    def scaled(a, s):
        return (scales[a, s] * ALPHA) * buf[a, s].astype(F32)

    def place(a, o):
        s = head[a, o]

        @pl.when(s < 0)
        def _():
            put(a, a + o, jnp.zeros((B, B), BF16))

        @pl.when(s >= 0)
        def _():
            rest = after[a, jnp.maximum(s, 0)]

            @pl.when(rest < 0)
            def _():
                put(a, a + o, scaled(a, s).astype(BF16))

            @pl.when(rest >= 0)
            def _():
                acc[...] = scaled(a, s)

                def more(t):
                    acc[...] = acc[...] + scaled(a, t)
                    return after[a, t]

                lax.while_loop(lambda t: t >= 0, more, rest)
                put(a, a + o, acc[...].astype(BF16))

    edge[rows(0), rows(1)] = jnp.zeros((B, B), BF16)
    edge[rows(3), rows(2)] = jnp.zeros((B, B), BF16)
    for a in range(ROWS):
        copies[a].wait()
        for o in range(SPAN):
            place(a, o)
    terms = dot(turned, edge[...]).T.astype(BF16)
    put_message(True, HANDED, terms[: 2 * B])
    put_message(False, HANDED, terms[2 * B :])


def first_local_kernel(own, edge, onsite, y0, diag, sym, edge_t, base):
    for a in range(ROWS):
        for b in range(a + 1):
            value = own[rows(a), rows(b)].astype(F32) + flip(own[rows(b), rows(a)])
            sym[rows(a), rows(b)] = value.astype(BF16)
            if b < a:
                sym[rows(b), rows(a)] = value.T.astype(BF16)
    for a in range(ROWS):
        for j in range(4):
            edge_t[rows(j), rows(a)] = flip(edge[rows(a), rows(j)]).astype(BF16)
    diag[...] = ALPHA * (onsite[...] - SHIFT)
    base[...] = diag[...] * y0[...].astype(F32) + dot(sym[...], y0[...])


def by_parity(body):
    parity = lax.rem(lax.axis_index(AXES), 2)
    for value in (0, 1):

        @pl.when(parity == value)
        def _(even=value == 0):
            body(even)


def from_right(a, edge, got, halo=0, terms=2 * B):
    wide = 1 if a == 0 else 2
    total = dot(edge[rows(a), rows(0, wide)], got[pl.ds(halo, wide * B), :])
    if a >= 2:
        total += got[pl.ds(terms + (a - 2) * B, B), :].astype(F32)
    return total


def from_left(a, edge, got, halo=0, terms=2 * B):
    skip = 1 if a == ROWS - 1 else 0
    total = dot(edge[rows(a), rows(2 + skip, 2 - skip)], got[pl.ds(halo + skip * B, (2 - skip) * B), :])
    if a < 2:
        total += got[pl.ds(terms + a * B, B), :].astype(F32)
    return total


def send_parts(edge_t, y, send_right, send_left):
    send_right[pl.ds(0, 2 * B), :] = y[pl.ds(2 * B, 2 * B), :]
    send_left[pl.ds(0, 2 * B), :] = y[pl.ds(0, 2 * B), :]
    send_right[pl.ds(2 * B, B), :] = dot(edge_t[rows(0), :], y[...]).astype(BF16)
    send_right[pl.ds(3 * B, B), :] = dot(edge_t[rows(1), rows(1, 3)], y[rows(1, 3), :]).astype(BF16)
    send_left[pl.ds(2 * B, B), :] = dot(edge_t[rows(2), rows(0, 3)], y[rows(0, 3), :]).astype(BF16)
    send_left[pl.ds(3 * B, B), :] = dot(edge_t[rows(3), :], y[...]).astype(BF16)


def first_post_kernel(base, edge_in, edge_t_in, to_e, to_o, got_e, got_o, edge, edge_t, y, send_e, send_o):
    edge[...] = edge_in[...]
    edge_t[...] = edge_t_in[...]

    def body(even):
        to_right, to_left = (to_e, to_o) if even else (to_o, to_e)
        got_right, got_left = (got_e, got_o) if even else (got_o, got_e)
        for i, (r, c) in enumerate(TO_LEFT):
            block = read_block(got_right, i).astype(F32)
            edge_t[rows(r), rows(c)] = (edge_t[rows(r), rows(c)].astype(F32) + block).astype(BF16)
            edge[rows(c), rows(r)] = (edge[rows(c), rows(r)].astype(F32) + block.T).astype(BF16)
        for i, (c, p) in enumerate(TO_RIGHT):
            block = read_block(got_left, i).astype(F32)
            r = p - 8
            edge_t[rows(c), rows(r)] = (edge_t[rows(c), rows(r)].astype(F32) + block).astype(BF16)
            edge[rows(r), rows(c)] = (edge[rows(r), rows(c)].astype(F32) + block.T).astype(BF16)
        halo = HANDED + 2 * B
        for a in range(ROWS):
            total = base[rows(a), :] + from_right(a, edge, got_right, halo, HANDED)
            total += from_left(a, edge, got_left, halo + 2 * B, HANDED)
            for places, source, got, start in ((TO_LEFT, to_left, got_left, 0), (TO_RIGHT, to_right, got_right, 8)):
                for i, (row, p) in enumerate(places):
                    if row == a:
                        total += dot(read_block(source, i), got[pl.ds(halo + (p - start) * B, B), :])
            y[rows(a), :] = (0.5 * total).astype(BF16)
        send_parts(edge_t, y, *((send_e, send_o) if even else (send_o, send_e)))

    by_parity(body)


def local_kernel(sym, diag, y, older, edge, got_e, base):
    base[...] = diag[...] * y[...].astype(F32) - older[...].astype(F32) + dot(sym[...], y[...])

    def body(even):
        for a in range(ROWS):
            base[rows(a), :] += (from_right if even else from_left)(a, edge, got_e)

    by_parity(body)


def receive(even, base, edge, got_o, y):
    for a in range(ROWS):
        y[rows(a), :] = (base[rows(a), :] + (from_left if even else from_right)(a, edge, got_o)).astype(BF16)


def post_kernel(base, edge, edge_t, got_o, y, send_e, send_o):
    def body(even):
        receive(even, base, edge, got_o, y)
        send_parts(edge_t, y, *((send_e, send_o) if even else (send_o, send_e)))

    by_parity(body)


def last_kernel(base, edge, got_o, y, gram):
    by_parity(lambda even: receive(even, base, edge, got_o, y))
    gram[...] = lax.dot_general(y[...], y[...], (((0,), (0,)), ((), ())), preferred_element_type=F32)


def lane_fill(x, c):
    return jnp.take_along_axis(x, jnp.full((T, K), c, jnp.int32), axis=1)


def row_fill(x, j):
    return jnp.take_along_axis(x, jnp.full((T, K), j, jnp.int32), axis=0)


def inverse_factor(gram, inverse):
    count = K // T
    lane = lax.broadcasted_iota(jnp.int32, (T, K), 1)
    sub = lax.broadcasted_iota(jnp.int32, (T, K), 0)
    tiles = [gram[pl.ds(T * t, T), :] for t in range(count)]
    for k in range(count):
        first = T * k
        inside = (lane >= first) & (lane < first + T)
        spread = [lane_fill(tiles[k], first + c) for c in range(T)]
        rest = jnp.where(inside, 0.0, tiles[k])
        steps = []
        scale = jnp.zeros((T, K), F32)
        for j in range(T):
            pivot = row_fill(spread[j], j)
            inv = 1.0 / pivot
            ratios = {c: row_fill(spread[c], j) * inv for c in range(j + 1, T)}
            row = jnp.where(lane == first + j, 1.0, row_fill(rest, j)) * inv
            steps.append((ratios, row))
            rest = rest - jnp.where(sub > j, spread[j], 0.0) * row
            for c in range(j + 1, T):
                spread[c] = spread[c] - spread[j] * ratios[c]
            scale = jnp.where(sub == j, lax.rsqrt(pivot), scale)
        unit = jnp.where(lane < first + sub, rest, jnp.where(lane == first + sub, 1.0, 0.0))
        inverse[pl.ds(first, T), :] = unit * scale
        for t in range(k + 1, count):
            factors = [lane_fill(tiles[t], first + c) for c in range(T)]
            value = jnp.where(inside, 0.0, tiles[t])
            for j, (ratios, row) in enumerate(steps):
                value = value - factors[j] * row
                for c in range(j + 1, T):
                    factors[c] = factors[c] - factors[j] * ratios[c]
            tiles[t] = value


def finish_kernel(scale, gram, y, basis, inverse):
    inverse_factor(gram, inverse)
    value = inverse[...] * scale
    high = value.astype(BF16)
    low = (value - high.astype(F32)).astype(BF16)
    dims = (((1,), (1,)), ((), ()))
    basis[...] = lax.dot_general(y[...], high, dims, preferred_element_type=F32) + lax.dot_general(
        y[...], low, dims, preferred_element_type=F32
    )


VMEM = pl.BlockSpec(memory_space=pltpu.VMEM)
SMEM = pl.BlockSpec(memory_space=pltpu.SMEM)
HBM = pl.BlockSpec(memory_space=pltpu.HBM)
LIMIT = 20 * 1024 * 1024
PREP_LIMIT = 57 * 1000 * 1000


def call(kernel, outs, specs, flops, size, scratch=(), aliases=None, limit=LIMIT):
    return pl.pallas_call(
        kernel,
        out_shape=[jax.ShapeDtypeStruct(*out) for out in outs],
        in_specs=list(specs),
        out_specs=[VMEM] * len(outs),
        scratch_shapes=list(scratch),
        input_output_aliases=aliases or {},
        cost_estimate=pl.CostEstimate(flops=flops, bytes_accessed=size, transcendentals=0),
        compiler_params=pltpu.CompilerParams(vmem_limit_bytes=limit),
    )


def swap_o(value):
    count = lax.axis_size(AXES)
    return lax.ppermute(value, AXES, [(i, (i + 1 if i % 2 else i - 1) % count) for i in range(count)])


def swap_e(value):
    return lax.ppermute(value, AXES, [(i, i ^ 1) for i in range(lax.axis_size(AXES))])


def group_sum(value, stride, size):
    count = lax.axis_size(AXES)
    parts = [value]
    for step in range(1, size):
        pairs = []
        for i in range(count):
            digit = (i // stride) % size
            partner = digit ^ step if size & (size - 1) == 0 else (digit + step) % size
            pairs.append((i, i + (partner - digit) * stride))
        parts.append(lax.ppermute(value, AXES, pairs))
    return sum(parts[1:], parts[0])


def digits():
    out, stride = [], 1
    for axis, cut in (("col", 4), ("row", 2)):
        left = lax.axis_size(axis)
        while left > 1:
            size = cut if left % cut == 0 else left
            out.append((stride, size))
            stride *= size
            left //= size
            cut = left if axis == "row" else cut
    return out


def local(blocks, block_scales, columns, live, onsite, start_vectors):
    slots = columns.shape[1]
    total = ROWS * lax.axis_size(AXES)
    column = ((OWN, 1), F32)
    tall = ((OWN, K), BF16)
    tall32 = ((OWN, K), F32)
    square = ((OWN, OWN), BF16)
    message = ((HANDED + 2 * B + OWN, K), BF16)
    product = 2 * OWN * OWN * K

    y0 = start_vectors
    own, edge, to_e, to_o = call(
        functools.partial(prep_kernel, total),
        [square, square, message, message],
        [SMEM, SMEM, SMEM, HBM, VMEM],
        product,
        10_000_000,
        [
            pltpu.VMEM((ROWS, slots, B, B), BF16),
            pltpu.VMEM((B, B), F32),
            pltpu.SMEM((ROWS, SPAN), jnp.int32),
            pltpu.SMEM((ROWS, slots), jnp.int32),
            pltpu.SemaphoreType.DMA((ROWS,)),
        ],
        limit=PREP_LIMIT,
    )(block_scales, columns, live, blocks, y0)
    got_o, got_e = swap_o(to_o), swap_e(to_e)
    diag, sym, edge_t, base = call(first_local_kernel, [column, square, square, tall32], [VMEM] * 4, product, 10_000_000)(
        own, edge, onsite[:, None], y0
    )
    edge, edge_t, y, send_e, send_o = call(
        first_post_kernel, [square, square, tall, tall, tall], [VMEM] * 7, 2 * product, 9_000_000, (), {1: 0, 2: 1}
    )(base, edge, edge_t, to_e, to_o, got_e, got_o)
    older = y0
    for step in range(1, DEG):
        got_o, got_e = swap_o(send_o), swap_e(send_e)
        base = call(local_kernel, [tall32], [VMEM] * 6, product, 3_500_000)(sym, diag, y, older, edge, got_e)[0]
        older = y
        if step < DEG - 1:
            y, send_e, send_o = call(post_kernel, [tall, tall, tall], [VMEM] * 4, 2 * product, 6_000_000)(
                base, edge, edge_t, got_o
            )
        else:
            y, gram = call(last_kernel, [tall, ((K, K), F32)], [VMEM] * 3, product, 4_000_000)(base, edge, got_o)
    for stride, size in digits():
        gram = group_sum(gram, stride, size)
    scale = float(np.sqrt(total * B))
    return call(
        functools.partial(finish_kernel, scale), [tall32], [VMEM] * 2, 2 * product, 1_000_000, [pltpu.VMEM((K, K), F32)]
    )(gram, y)[0]


def solution(mesh):
    return jax.shard_map(
        local,
        mesh=mesh,
        in_specs=(
            P(AXES, None, None, None),
            P(AXES, None),
            P(AXES, None),
            P(AXES),
            P(AXES),
            P(AXES, None),
        ),
        out_specs=P(AXES, None),
        check_vma=False,
    )
```

```python
import functools

import jax
import jax.numpy as jnp
import numpy as np
from jax import lax
from jax.experimental import pallas as pl
from jax.experimental.pallas import tpu as pltpu
from jax.sharding import PartitionSpec as P

DEG = 5
B = 256
K = 128
ROWS = 4
OWN = ROWS * B
REACH = 4
SPAN = 2 * REACH + 1
AXES = ("row", "col")
ALPHA = 2.0 / 1.1
SHIFT = 0.2
F32 = jnp.float32
BF16 = jnp.bfloat16
EDGE = (8, 9, 2, 3)
TO_RIGHT = ((2, 10), (3, 10), (3, 11))
TO_LEFT = ((0, 0), (0, 1), (1, 1))
HANDED = 3 * 2 * B
T = 8


def rows(i, n=1):
    return pl.ds(i * B, n * B)


def dot(a, b):
    return jnp.dot(a, b, preferred_element_type=F32)


def read_block(ref, i):
    return jnp.concatenate([ref[rows(2 * i), :], ref[rows(2 * i + 1), :]], axis=1)


def flip(block):
    return block.astype(F32).T


def prep_kernel(total, scales_in, columns_in, live_in, blocks, y0, own_out, edge_out, to_e, to_o, buf, acc, own, edge, msg, y0_in, scales, columns, live, head, after, sem, sent):
    small = [
        pltpu.make_async_copy(source, target, sent.at[15 + i])
        for i, (source, target) in enumerate(((live_in, live), (columns_in, columns), (scales_in, scales)))
    ]
    for copy in small:
        copy.start()
    start_y0 = pltpu.make_async_copy(y0, y0_in, sent.at[12])
    start_y0.start()
    copies = [pltpu.make_async_copy(blocks.at[a], buf.at[a], sem.at[a]) for a in range(ROWS)]
    for copy in copies:
        copy.start()
    even = lax.rem(lax.axis_index(AXES), 2) == 0
    first = lax.axis_index(AXES) * ROWS
    for copy in small:
        copy.wait()
    for a in range(ROWS):
        for o in range(SPAN):
            head[a, o] = -1

        def chain(s, carry, a=a):
            o = lax.rem(columns[a, s] - (first + a) + REACH + total, total)
            after[a, s] = head[a, o]
            head[a, o] = s
            return carry

        lax.fori_loop(0, live[a], chain, 0)
    start_y0.wait()
    waits = []
    for i, target in enumerate((to_e, to_o)):
        copy = pltpu.make_async_copy(y0_in, target.at[pl.ds(HANDED + 2 * B, OWN), :], sent.at[10 + i])
        copy.start()
        waits.append(copy)
    turned = flip(y0_in[...]).astype(BF16)

    def post_message(right, start, count, slot):
        side = 0 if right else 1
        part = pl.ds(start, count)

        @pl.when(even == right)
        def _():
            pltpu.make_async_copy(msg.at[side, part, :], to_e.at[part, :], sent.at[slot]).start()

        @pl.when(even != right)
        def _():
            pltpu.make_async_copy(msg.at[side, part, :], to_o.at[part, :], sent.at[slot]).start()

        waits.append(pltpu.make_async_copy(msg.at[side, part, :], to_e.at[part, :], sent.at[slot]))

    def put(a, p, value):
        if 4 <= p < 8:
            own[rows(a), rows(p - 4)] = value
        elif p in EDGE:
            edge[rows(a), rows(EDGE.index(p))] = value
        else:
            side, places = (0, TO_RIGHT) if p > 8 else (1, TO_LEFT)
            i = places.index((a, p))
            msg[side, rows(2 * i), :] = value[:, :K]
            msg[side, rows(2 * i + 1), :] = value[:, K:]

    def scaled(a, s):
        return (scales[a, s] * ALPHA) * buf[a, s].astype(F32)

    def place(a, o):
        s = head[a, o]

        @pl.when(s < 0)
        def _():
            put(a, a + o, jnp.zeros((B, B), BF16))

        @pl.when(s >= 0)
        def _():
            rest = after[a, jnp.maximum(s, 0)]

            @pl.when(rest < 0)
            def _():
                put(a, a + o, scaled(a, s).astype(BF16))

            last = after[a, jnp.maximum(rest, 0)]

            @pl.when((rest >= 0) & (last < 0))
            def _():
                put(a, a + o, (scaled(a, s) + scaled(a, rest)).astype(BF16))

            @pl.when((rest >= 0) & (last >= 0))
            def _():
                acc[...] = scaled(a, s)

                def more(t):
                    acc[...] = acc[...] + scaled(a, t)
                    return after[a, t]

                lax.while_loop(lambda t: t >= 0, more, rest)
                put(a, a + o, acc[...].astype(BF16))

    edge[rows(0), rows(1)] = jnp.zeros((B, B), BF16)
    edge[rows(3), rows(2)] = jnp.zeros((B, B), BF16)
    for a in range(ROWS):
        copies[a].wait()
        for o in range(SPAN):
            place(a, o)
        for i, (source, target) in enumerate(((own, own_out), (edge, edge_out))):
            copy = pltpu.make_async_copy(source.at[rows(a), :], target.at[rows(a), :], sent.at[4 * i + a])
            copy.start()
            waits.append(copy)
        if a % 2 == 1:
            post_message(a == 3, 0, HANDED, 8 if a == 3 else 9)
    terms = dot(turned, edge[...]).T.astype(BF16)
    msg[0, pl.ds(HANDED, 2 * B), :] = terms[: 2 * B]
    msg[1, pl.ds(HANDED, 2 * B), :] = terms[2 * B :]
    post_message(True, HANDED, 2 * B, 13)
    post_message(False, HANDED, 2 * B, 14)
    for copy in waits:
        copy.wait()


def first_local_kernel(own, edge, onsite, y0, diag, sym, edge_t, base):
    for a in range(ROWS):
        for b in range(a + 1):
            value = own[rows(a), rows(b)].astype(F32) + flip(own[rows(b), rows(a)])
            sym[rows(a), rows(b)] = value.astype(BF16)
            if b < a:
                sym[rows(b), rows(a)] = value.T.astype(BF16)
    for a in range(ROWS):
        for j in range(4):
            edge_t[rows(j), rows(a)] = flip(edge[rows(a), rows(j)]).astype(BF16)
    diag[...] = ALPHA * (onsite[...] - SHIFT)
    base[...] = diag[...] * y0[...].astype(F32) + dot(sym[...], y0[...])


def by_parity(body):
    parity = lax.rem(lax.axis_index(AXES), 2)
    for value in (0, 1):

        @pl.when(parity == value)
        def _(even=value == 0):
            body(even)


def from_right(a, edge, got, halo=0, terms=2 * B):
    wide = 1 if a == 0 else 2
    total = dot(edge[rows(a), rows(0, wide)], got[pl.ds(halo, wide * B), :])
    if a >= 2:
        total += got[pl.ds(terms + (a - 2) * B, B), :].astype(F32)
    return total


def from_left(a, edge, got, halo=0, terms=2 * B):
    skip = 1 if a == ROWS - 1 else 0
    total = dot(edge[rows(a), rows(2 + skip, 2 - skip)], got[pl.ds(halo + skip * B, (2 - skip) * B), :])
    if a < 2:
        total += got[pl.ds(terms + a * B, B), :].astype(F32)
    return total


def send_parts(edge_t, y, send_right, send_left):
    send_right[pl.ds(0, 2 * B), :] = y[pl.ds(2 * B, 2 * B), :]
    send_left[pl.ds(0, 2 * B), :] = y[pl.ds(0, 2 * B), :]
    send_right[pl.ds(2 * B, B), :] = dot(edge_t[rows(0), :], y[...]).astype(BF16)
    send_right[pl.ds(3 * B, B), :] = dot(edge_t[rows(1), rows(1, 3)], y[rows(1, 3), :]).astype(BF16)
    send_left[pl.ds(2 * B, B), :] = dot(edge_t[rows(2), rows(0, 3)], y[rows(0, 3), :]).astype(BF16)
    send_left[pl.ds(3 * B, B), :] = dot(edge_t[rows(3), :], y[...]).astype(BF16)


def first_post_kernel(base, edge_in, edge_t_in, to_e, to_o, got_e, got_o, edge, edge_t, y, send_e, send_o):
    edge[...] = edge_in[...]
    edge_t[...] = edge_t_in[...]

    def body(even):
        to_right, to_left = (to_e, to_o) if even else (to_o, to_e)
        got_right, got_left = (got_e, got_o) if even else (got_o, got_e)
        for i, (r, c) in enumerate(TO_LEFT):
            block = read_block(got_right, i).astype(F32)
            edge_t[rows(r), rows(c)] = (edge_t[rows(r), rows(c)].astype(F32) + block).astype(BF16)
            edge[rows(c), rows(r)] = (edge[rows(c), rows(r)].astype(F32) + block.T).astype(BF16)
        for i, (c, p) in enumerate(TO_RIGHT):
            block = read_block(got_left, i).astype(F32)
            r = p - 8
            edge_t[rows(c), rows(r)] = (edge_t[rows(c), rows(r)].astype(F32) + block).astype(BF16)
            edge[rows(r), rows(c)] = (edge[rows(r), rows(c)].astype(F32) + block.T).astype(BF16)
        halo = HANDED + 2 * B
        for a in range(ROWS):
            total = base[rows(a), :] + from_right(a, edge, got_right, halo, HANDED)
            total += from_left(a, edge, got_left, halo + 2 * B, HANDED)
            for places, source, got, start in ((TO_LEFT, to_left, got_left, 0), (TO_RIGHT, to_right, got_right, 8)):
                for i, (row, p) in enumerate(places):
                    if row == a:
                        total += dot(read_block(source, i), got[pl.ds(halo + (p - start) * B, B), :])
            y[rows(a), :] = (0.5 * total).astype(BF16)
        send_parts(edge_t, y, *((send_e, send_o) if even else (send_o, send_e)))

    by_parity(body)


def local_kernel(sym, diag, y, older, edge, got_e, base):
    base[...] = diag[...] * y[...].astype(F32) - older[...].astype(F32) + dot(sym[...], y[...])

    def body(even):
        for a in range(ROWS):
            base[rows(a), :] += (from_right if even else from_left)(a, edge, got_e)

    by_parity(body)


def receive(even, base, edge, got_o, y):
    for a in range(ROWS):
        y[rows(a), :] = (base[rows(a), :] + (from_left if even else from_right)(a, edge, got_o)).astype(BF16)


def post_kernel(base, edge, edge_t, got_o, y, send_e, send_o):
    def body(even):
        receive(even, base, edge, got_o, y)
        send_parts(edge_t, y, *((send_e, send_o) if even else (send_o, send_e)))

    by_parity(body)


def last_kernel(base, edge, got_o, y, gram):
    by_parity(lambda even: receive(even, base, edge, got_o, y))
    gram[...] = lax.dot_general(y[...], y[...], (((0,), (0,)), ((), ())), preferred_element_type=F32)


def lane_fill(x, c):
    return jnp.take_along_axis(x, jnp.full((T, K), c, jnp.int32), axis=1)


def row_fill(x, j):
    return jnp.take_along_axis(x, jnp.full((T, K), j, jnp.int32), axis=0)


def inverse_factor(gram, inverse):
    count = K // T
    lane = lax.broadcasted_iota(jnp.int32, (T, K), 1)
    sub = lax.broadcasted_iota(jnp.int32, (T, K), 0)
    tiles = [gram[pl.ds(T * t, T), :] for t in range(count)]
    for k in range(count):
        first = T * k
        inside = (lane >= first) & (lane < first + T)
        spread = [lane_fill(tiles[k], first + c) for c in range(T)]
        rest = jnp.where(inside, 0.0, tiles[k])
        steps = []
        scale = jnp.zeros((T, K), F32)
        for j in range(T):
            pivot = row_fill(spread[j], j)
            inv = 1.0 / pivot
            ratios = {c: row_fill(spread[c], j) * inv for c in range(j + 1, T)}
            row = jnp.where(lane == first + j, 1.0, row_fill(rest, j)) * inv
            steps.append((ratios, row))
            rest = rest - jnp.where(sub > j, spread[j], 0.0) * row
            for c in range(j + 1, T):
                spread[c] = spread[c] - spread[j] * ratios[c]
            scale = jnp.where(sub == j, lax.rsqrt(pivot), scale)
        unit = jnp.where(lane < first + sub, rest, jnp.where(lane == first + sub, 1.0, 0.0))
        inverse[pl.ds(first, T), :] = unit * scale
        for t in range(k + 1, count):
            factors = [lane_fill(tiles[t], first + c) for c in range(T)]
            value = jnp.where(inside, 0.0, tiles[t])
            for j, (ratios, row) in enumerate(steps):
                value = value - factors[j] * row
                for c in range(j + 1, T):
                    factors[c] = factors[c] - factors[j] * ratios[c]
            tiles[t] = value


def finish_kernel(scale, gram, y, basis, inverse):
    inverse_factor(gram, inverse)
    value = inverse[...] * scale
    high = value.astype(BF16)
    low = (value - high.astype(F32)).astype(BF16)
    dims = (((1,), (1,)), ((), ()))
    basis[...] = lax.dot_general(y[...], high, dims, preferred_element_type=F32) + lax.dot_general(
        y[...], low, dims, preferred_element_type=F32
    )


VMEM = pl.BlockSpec(memory_space=pltpu.VMEM)
SMEM = pl.BlockSpec(memory_space=pltpu.SMEM)
HBM = pl.BlockSpec(memory_space=pltpu.HBM)
LIMIT = 20 * 1024 * 1024
PREP_LIMIT = 57 * 1000 * 1000


def call(kernel, outs, specs, flops, size, scratch=(), aliases=None, limit=LIMIT, out_spec=None):
    return pl.pallas_call(
        kernel,
        out_shape=[jax.ShapeDtypeStruct(*out) for out in outs],
        in_specs=list(specs),
        out_specs=[out_spec or VMEM] * len(outs),
        scratch_shapes=list(scratch),
        input_output_aliases=aliases or {},
        cost_estimate=pl.CostEstimate(flops=flops, bytes_accessed=size, transcendentals=0),
        compiler_params=pltpu.CompilerParams(vmem_limit_bytes=limit),
    )


def swap_o(value):
    count = lax.axis_size(AXES)
    return lax.ppermute(value, AXES, [(i, (i + 1 if i % 2 else i - 1) % count) for i in range(count)])


def swap_e(value):
    return lax.ppermute(value, AXES, [(i, i ^ 1) for i in range(lax.axis_size(AXES))])


def group_sum(value, stride, size):
    count = lax.axis_size(AXES)
    parts = [value]
    for step in range(1, size):
        pairs = []
        for i in range(count):
            digit = (i // stride) % size
            partner = digit ^ step if size & (size - 1) == 0 else (digit + step) % size
            pairs.append((i, i + (partner - digit) * stride))
        parts.append(lax.ppermute(value, AXES, pairs))
    return sum(parts[1:], parts[0])


def digits():
    out, stride = [], 1
    for axis, cut in (("col", 4), ("row", 2)):
        left = lax.axis_size(axis)
        while left > 1:
            size = cut if left % cut == 0 else left
            out.append((stride, size))
            stride *= size
            left //= size
            cut = left if axis == "row" else cut
    return out


def local(blocks, block_scales, columns, live, onsite, start_vectors):
    slots = columns.shape[1]
    total = ROWS * lax.axis_size(AXES)
    column = ((OWN, 1), F32)
    tall = ((OWN, K), BF16)
    tall32 = ((OWN, K), F32)
    square = ((OWN, OWN), BF16)
    message = ((HANDED + 2 * B + OWN, K), BF16)
    product = 2 * OWN * OWN * K

    y0 = start_vectors
    own, edge, to_e, to_o = call(
        functools.partial(prep_kernel, total),
        [square, square, message, message],
        [HBM] * 5,
        product,
        10_000_000,
        [
            pltpu.VMEM((ROWS, slots, B, B), BF16),
            pltpu.VMEM((B, B), F32),
            pltpu.VMEM((OWN, OWN), BF16),
            pltpu.VMEM((OWN, OWN), BF16),
            pltpu.VMEM((2, HANDED + 2 * B, K), BF16),
            pltpu.VMEM((OWN, K), BF16),
            pltpu.SMEM((ROWS, slots), F32),
            pltpu.SMEM((ROWS, slots), jnp.int32),
            pltpu.SMEM((ROWS,), jnp.int32),
            pltpu.SMEM((ROWS, SPAN), jnp.int32),
            pltpu.SMEM((ROWS, slots), jnp.int32),
            pltpu.SemaphoreType.DMA((ROWS,)),
            pltpu.SemaphoreType.DMA((18,)),
        ],
        out_spec=HBM,
        limit=PREP_LIMIT,
    )(block_scales, columns, live, blocks, y0)
    got_o, got_e = swap_o(to_o), swap_e(to_e)
    diag, sym, edge_t, base = call(first_local_kernel, [column, square, square, tall32], [VMEM] * 4, product, 10_000_000)(
        own, edge, onsite[:, None], y0
    )
    edge, edge_t, y, send_e, send_o = call(
        first_post_kernel, [square, square, tall, tall, tall], [VMEM] * 7, 2 * product, 9_000_000, (), {1: 0, 2: 1}
    )(base, edge, edge_t, to_e, to_o, got_e, got_o)
    older = y0
    for step in range(1, DEG):
        got_o, got_e = swap_o(send_o), swap_e(send_e)
        base = call(local_kernel, [tall32], [VMEM] * 6, product, 3_500_000)(sym, diag, y, older, edge, got_e)[0]
        older = y
        if step < DEG - 1:
            y, send_e, send_o = call(post_kernel, [tall, tall, tall], [VMEM] * 4, 2 * product, 6_000_000)(
                base, edge, edge_t, got_o
            )
        else:
            y, gram = call(last_kernel, [tall, ((K, K), F32)], [VMEM] * 3, product, 4_000_000)(base, edge, got_o)
    for stride, size in digits():
        gram = group_sum(gram, stride, size)
    scale = float(np.sqrt(total * B))
    return call(
        functools.partial(finish_kernel, scale), [tall32], [VMEM] * 2, 2 * product, 1_000_000, [pltpu.VMEM((K, K), F32)]
    )(gram, y)[0]


def solution(mesh):
    return jax.shard_map(
        local,
        mesh=mesh,
        in_specs=(
            P(AXES, None, None, None),
            P(AXES, None),
            P(AXES, None),
            P(AXES),
            P(AXES),
            P(AXES, None),
        ),
        out_specs=P(AXES, None),
        check_vma=False,
    )
```

```python
import functools

import jax
import jax.numpy as jnp
import numpy as np
from jax import lax
from jax.experimental import pallas as pl
from jax.experimental.pallas import tpu as pltpu
from jax.sharding import PartitionSpec as P

DEG = 5
B = 256
K = 128
ROWS = 4
OWN = ROWS * B
REACH = 4
SPAN = 2 * REACH + 1
AXES = ("row", "col")
ALPHA = 2.0 / 1.1
SHIFT = 0.2
F32 = jnp.float32
BF16 = jnp.bfloat16
EDGE = (8, 9, 2, 3)
TO_RIGHT = ((2, 10), (3, 10), (3, 11))
TO_LEFT = ((0, 0), (0, 1), (1, 1))
HANDED = 3 * 2 * B
T = 8


def rows(i, n=1):
    return pl.ds(i * B, n * B)


def dot(a, b):
    return jnp.dot(a, b, preferred_element_type=F32)


def read_block(ref, i):
    return jnp.concatenate([ref[rows(2 * i), :], ref[rows(2 * i + 1), :]], axis=1)


def flip(block):
    return block.astype(F32).T


def prep_kernel(total, scales_in, columns_in, live_in, blocks, y0, own_out, edge_out, to_e, to_o, buf, acc, own, edge, msg, y0_in, scales, columns, live, head, after, sem, sent):
    small = [
        pltpu.make_async_copy(source, target, sent.at[15 + i])
        for i, (source, target) in enumerate(((live_in, live), (columns_in, columns), (scales_in, scales)))
    ]
    for copy in small:
        copy.start()
    start_y0 = pltpu.make_async_copy(y0, y0_in, sent.at[12])
    start_y0.start()
    copies = [pltpu.make_async_copy(blocks.at[a], buf.at[a], sem.at[a]) for a in range(ROWS)]
    for copy in copies:
        copy.start()
    even = lax.rem(lax.axis_index(AXES), 2) == 0
    first = lax.axis_index(AXES) * ROWS
    for copy in small:
        copy.wait()
    for a in range(ROWS):
        for o in range(SPAN):
            head[a, o] = -1

        def chain(s, carry, a=a):
            o = lax.rem(columns[a, s] - (first + a) + REACH + total, total)
            after[a, s] = head[a, o]
            head[a, o] = s
            return carry

        lax.fori_loop(0, live[a], chain, 0)
    start_y0.wait()
    waits = []
    for i, target in enumerate((to_e, to_o)):
        copy = pltpu.make_async_copy(y0_in, target.at[pl.ds(HANDED + 2 * B, OWN), :], sent.at[10 + i])
        copy.start()
        waits.append(copy)
    turned = flip(y0_in[...]).astype(BF16)

    def post_message(right, start, count, slot):
        side = 0 if right else 1
        part = pl.ds(start, count)

        @pl.when(even == right)
        def _():
            pltpu.make_async_copy(msg.at[side, part, :], to_e.at[part, :], sent.at[slot]).start()

        @pl.when(even != right)
        def _():
            pltpu.make_async_copy(msg.at[side, part, :], to_o.at[part, :], sent.at[slot]).start()

        waits.append(pltpu.make_async_copy(msg.at[side, part, :], to_e.at[part, :], sent.at[slot]))

    def put(a, p, value):
        if 4 <= p < 8:
            own[rows(a), rows(p - 4)] = value
        elif p in EDGE:
            edge[rows(a), rows(EDGE.index(p))] = value
        else:
            side, places = (0, TO_RIGHT) if p > 8 else (1, TO_LEFT)
            i = places.index((a, p))
            msg[side, rows(2 * i), :] = value[:, :K]
            msg[side, rows(2 * i + 1), :] = value[:, K:]

    def scaled(a, s):
        return (scales[a, s] * ALPHA) * buf[a, s].astype(F32)

    def place(a, o):
        s = head[a, o]

        @pl.when(s < 0)
        def _():
            put(a, a + o, jnp.zeros((B, B), BF16))

        @pl.when(s >= 0)
        def _():
            rest = after[a, jnp.maximum(s, 0)]

            @pl.when(rest < 0)
            def _():
                put(a, a + o, scaled(a, s).astype(BF16))

            last = after[a, jnp.maximum(rest, 0)]

            @pl.when((rest >= 0) & (last < 0))
            def _():
                put(a, a + o, (scaled(a, s) + scaled(a, rest)).astype(BF16))

            @pl.when((rest >= 0) & (last >= 0))
            def _():
                acc[...] = scaled(a, s)

                def more(t):
                    acc[...] = acc[...] + scaled(a, t)
                    return after[a, t]

                lax.while_loop(lambda t: t >= 0, more, rest)
                put(a, a + o, acc[...].astype(BF16))

    edge[rows(0), rows(1)] = jnp.zeros((B, B), BF16)
    edge[rows(3), rows(2)] = jnp.zeros((B, B), BF16)
    for a in range(ROWS):
        copies[a].wait()
        for o in range(SPAN):
            place(a, o)
        for i, (source, target) in enumerate(((own, own_out), (edge, edge_out))):
            copy = pltpu.make_async_copy(source.at[rows(a), :], target.at[rows(a), :], sent.at[4 * i + a])
            copy.start()
            waits.append(copy)
        if a % 2 == 1:
            post_message(a == 3, 0, HANDED, 8 if a == 3 else 9)
    terms = dot(turned, edge[...]).T.astype(BF16)
    msg[0, pl.ds(HANDED, 2 * B), :] = terms[: 2 * B]
    msg[1, pl.ds(HANDED, 2 * B), :] = terms[2 * B :]
    post_message(True, HANDED, 2 * B, 13)
    post_message(False, HANDED, 2 * B, 14)
    for copy in waits:
        copy.wait()


def first_local_kernel(own, edge, onsite, y0, diag, sym, edge_t, base):
    for a in range(ROWS):
        for b in range(a + 1):
            value = own[rows(a), rows(b)].astype(F32) + flip(own[rows(b), rows(a)])
            sym[rows(a), rows(b)] = value.astype(BF16)
            if b < a:
                sym[rows(b), rows(a)] = value.T.astype(BF16)
    for a in range(ROWS):
        for j in range(4):
            edge_t[rows(j), rows(a)] = flip(edge[rows(a), rows(j)]).astype(BF16)
    diag[...] = ALPHA * (onsite[...] - SHIFT)
    base[...] = diag[...] * y0[...].astype(F32) + dot(sym[...], y0[...])


def by_parity(body):
    parity = lax.rem(lax.axis_index(AXES), 2)
    for value in (0, 1):

        @pl.when(parity == value)
        def _(even=value == 0):
            body(even)


def halo_right(a, edge, got, halo=0):
    wide = 1 if a == 0 else 2
    return dot(edge[rows(a), rows(0, wide)], got[pl.ds(halo, wide * B), :])


def halo_left(a, edge, got, halo=0):
    skip = 1 if a == ROWS - 1 else 0
    return dot(edge[rows(a), rows(2 + skip, 2 - skip)], got[pl.ds(halo + skip * B, (2 - skip) * B), :])


def terms_of(a, got_left, got_right, start=0):
    got = got_left if a < 2 else got_right
    return got[pl.ds(start + (a % 2) * B, B), :].astype(F32)


HALF = K // 2


def half_mask(half):
    lane = lax.broadcasted_iota(jnp.int32, (B, K), 1)
    return (lane < HALF) if half == 0 else (lane >= HALF)


def take(sides, got_e, got_o):
    parity = lax.rem(lax.axis_index(AXES), 2)
    sides[parity] = got_e[...]
    sides[1 - parity] = got_o[...]


def give(sides, send_e, send_o):
    parity = lax.rem(lax.axis_index(AXES), 2)
    send_e[...] = sides[parity]
    send_o[...] = sides[1 - parity]


def pack(half, edge_t, y, sides, spare):
    mine = half_mask(half)
    for a in range(ROWS):
        value = jnp.where(mine, y[rows(a), :].astype(F32), 0.0)
        spare[rows(a), :] = pltpu.roll(value, HALF, 1).astype(BF16)

    def put(side, i, row, terms):
        sides[side, rows(i), :] = jnp.where(mine, y[rows(row), :].astype(F32), terms).astype(BF16)

    put(0, 0, 2, dot(edge_t[rows(0), :], spare[...]))
    put(0, 1, 3, dot(edge_t[rows(1), rows(1, 3)], spare[rows(1, 3), :]))
    put(1, 0, 0, dot(edge_t[rows(2), rows(0, 3)], spare[rows(0, 3), :]))
    put(1, 1, 1, dot(edge_t[rows(3), :], spare[...]))


def first_post_kernel(base, edge_in, edge_t_in, to_e, to_o, got_e, got_o, edge, edge_t, y, send_e, send_o, send_e2, send_o2, spare, sides):
    edge[...] = edge_in[...]
    edge_t[...] = edge_t_in[...]

    def body(even):
        to_right, to_left = (to_e, to_o) if even else (to_o, to_e)
        got_right, got_left = (got_e, got_o) if even else (got_o, got_e)
        for i, (r, c) in enumerate(TO_LEFT):
            block = read_block(got_right, i).astype(F32)
            edge_t[rows(r), rows(c)] = (edge_t[rows(r), rows(c)].astype(F32) + block).astype(BF16)
            edge[rows(c), rows(r)] = (edge[rows(c), rows(r)].astype(F32) + block.T).astype(BF16)
        for i, (c, p) in enumerate(TO_RIGHT):
            block = read_block(got_left, i).astype(F32)
            r = p - 8
            edge_t[rows(c), rows(r)] = (edge_t[rows(c), rows(r)].astype(F32) + block).astype(BF16)
            edge[rows(r), rows(c)] = (edge[rows(r), rows(c)].astype(F32) + block.T).astype(BF16)
        halo = HANDED + 2 * B
        for a in range(ROWS):
            total = base[rows(a), :] + halo_right(a, edge, got_right, halo)
            total += halo_left(a, edge, got_left, halo + 2 * B) + terms_of(a, got_left, got_right, HANDED)
            for places, source, got, start in ((TO_LEFT, to_left, got_left, 0), (TO_RIGHT, to_right, got_right, 8)):
                for i, (row, p) in enumerate(places):
                    if row == a:
                        total += dot(read_block(source, i), got[pl.ds(halo + (p - start) * B, B), :])
            y[rows(a), :] = (0.5 * total).astype(BF16)
    by_parity(body)
    for half, to_e, to_o in ((0, send_e, send_o), (1, send_e2, send_o2)):
        pack(half, edge_t, y, sides, spare)
        give(sides, to_e, to_o)


def local_kernel(sym, diag, y, older, base):
    base[...] = diag[...] * y[...].astype(F32) - older[...].astype(F32) + dot(sym[...], y[...])


def receive(half, base, edge, got_e, got_o, y_in, y, sides):
    take(sides, got_e, got_o)
    right, left = sides.at[0], sides.at[1]
    for a in range(ROWS):
        total = base[rows(a), :] + halo_right(a, edge, right) + halo_left(a, edge, left)
        total += pltpu.roll(terms_of(a, left, right), HALF, 1)
        y[rows(a), :] = jnp.where(half_mask(half), total, y_in[rows(a), :].astype(F32)).astype(BF16)


def post_kernel(half, base, edge, edge_t, got_e, got_o, y_in, y, send_e, send_o, spare, sides):
    receive(half, base, edge, got_e, got_o, y_in, y, sides)
    pack(half, edge_t, y, sides, spare)
    give(sides, send_e, send_o)


def last_first_kernel(base, edge, got_e, got_o, y_in, y, sides):
    receive(0, base, edge, got_e, got_o, y_in, y, sides)


def last_kernel(base, edge, got_e, got_o, y_in, y, gram, sides):
    receive(1, base, edge, got_e, got_o, y_in, y, sides)
    gram[...] = lax.dot_general(y[...], y[...], (((0,), (0,)), ((), ())), preferred_element_type=F32)


def lane_fill(x, c):
    return jnp.take_along_axis(x, jnp.full((T, K), c, jnp.int32), axis=1)


def row_fill(x, j):
    return jnp.take_along_axis(x, jnp.full((T, K), j, jnp.int32), axis=0)


def inverse_factor(gram, inverse):
    count = K // T
    lane = lax.broadcasted_iota(jnp.int32, (T, K), 1)
    sub = lax.broadcasted_iota(jnp.int32, (T, K), 0)
    tiles = [gram[pl.ds(T * t, T), :] for t in range(count)]
    for k in range(count):
        first = T * k
        inside = (lane >= first) & (lane < first + T)
        spread = [lane_fill(tiles[k], first + c) for c in range(T)]
        rest = jnp.where(inside, 0.0, tiles[k])
        steps = []
        scale = jnp.zeros((T, K), F32)
        for j in range(T):
            pivot = row_fill(spread[j], j)
            inv = 1.0 / pivot
            ratios = {c: row_fill(spread[c], j) * inv for c in range(j + 1, T)}
            row = jnp.where(lane == first + j, 1.0, row_fill(rest, j)) * inv
            steps.append((ratios, row))
            rest = rest - jnp.where(sub > j, spread[j], 0.0) * row
            for c in range(j + 1, T):
                spread[c] = spread[c] - spread[j] * ratios[c]
            scale = jnp.where(sub == j, lax.rsqrt(pivot), scale)
        unit = jnp.where(lane < first + sub, rest, jnp.where(lane == first + sub, 1.0, 0.0))
        inverse[pl.ds(first, T), :] = unit * scale
        for t in range(k + 1, count):
            factors = [lane_fill(tiles[t], first + c) for c in range(T)]
            value = jnp.where(inside, 0.0, tiles[t])
            for j, (ratios, row) in enumerate(steps):
                value = value - factors[j] * row
                for c in range(j + 1, T):
                    factors[c] = factors[c] - factors[j] * ratios[c]
            tiles[t] = value


def finish_kernel(scale, gram, y, basis, inverse):
    inverse_factor(gram, inverse)
    value = inverse[...] * scale
    high = value.astype(BF16)
    low = (value - high.astype(F32)).astype(BF16)
    dims = (((1,), (1,)), ((), ()))
    basis[...] = lax.dot_general(y[...], high, dims, preferred_element_type=F32) + lax.dot_general(
        y[...], low, dims, preferred_element_type=F32
    )


VMEM = pl.BlockSpec(memory_space=pltpu.VMEM)
SMEM = pl.BlockSpec(memory_space=pltpu.SMEM)
HBM = pl.BlockSpec(memory_space=pltpu.HBM)
LIMIT = 20 * 1024 * 1024
PREP_LIMIT = 57 * 1000 * 1000


def call(kernel, outs, specs, flops, size, scratch=(), aliases=None, limit=LIMIT, out_spec=None):
    return pl.pallas_call(
        kernel,
        out_shape=[jax.ShapeDtypeStruct(*out) for out in outs],
        in_specs=list(specs),
        out_specs=[out_spec or VMEM] * len(outs),
        scratch_shapes=list(scratch),
        input_output_aliases=aliases or {},
        cost_estimate=pl.CostEstimate(flops=flops, bytes_accessed=size, transcendentals=0),
        compiler_params=pltpu.CompilerParams(vmem_limit_bytes=limit),
    )


def swap_o(value):
    count = lax.axis_size(AXES)
    return lax.ppermute(value, AXES, [(i, (i + 1 if i % 2 else i - 1) % count) for i in range(count)])


def swap_e(value):
    return lax.ppermute(value, AXES, [(i, i ^ 1) for i in range(lax.axis_size(AXES))])


def exchange(send_e, send_o):
    got_o = swap_o(send_o)
    return swap_e(send_e), got_o


def group_sum(value, stride, size):
    count = lax.axis_size(AXES)
    parts = [value]
    for step in range(1, size):
        pairs = []
        for i in range(count):
            digit = (i // stride) % size
            partner = digit ^ step if size & (size - 1) == 0 else (digit + step) % size
            pairs.append((i, i + (partner - digit) * stride))
        parts.append(lax.ppermute(value, AXES, pairs))
    return sum(parts[1:], parts[0])


def digits():
    out, stride = [], 1
    for axis, cut in (("col", 4), ("row", 2)):
        left = lax.axis_size(axis)
        while left > 1:
            size = cut if left % cut == 0 else left
            out.append((stride, size))
            stride *= size
            left //= size
            cut = left if axis == "row" else cut
    return out


def local(blocks, block_scales, columns, live, onsite, start_vectors):
    slots = columns.shape[1]
    total = ROWS * lax.axis_size(AXES)
    column = ((OWN, 1), F32)
    tall = ((OWN, K), BF16)
    tall32 = ((OWN, K), F32)
    square = ((OWN, OWN), BF16)
    message = ((HANDED + 2 * B + OWN, K), BF16)
    product = 2 * OWN * OWN * K

    y0 = start_vectors
    own, edge, to_e, to_o = call(
        functools.partial(prep_kernel, total),
        [square, square, message, message],
        [HBM] * 5,
        product,
        10_000_000,
        [
            pltpu.VMEM((ROWS, slots, B, B), BF16),
            pltpu.VMEM((B, B), F32),
            pltpu.VMEM((OWN, OWN), BF16),
            pltpu.VMEM((OWN, OWN), BF16),
            pltpu.VMEM((2, HANDED + 2 * B, K), BF16),
            pltpu.VMEM((OWN, K), BF16),
            pltpu.SMEM((ROWS, slots), F32),
            pltpu.SMEM((ROWS, slots), jnp.int32),
            pltpu.SMEM((ROWS,), jnp.int32),
            pltpu.SMEM((ROWS, SPAN), jnp.int32),
            pltpu.SMEM((ROWS, slots), jnp.int32),
            pltpu.SemaphoreType.DMA((ROWS,)),
            pltpu.SemaphoreType.DMA((18,)),
        ],
        out_spec=HBM,
        limit=PREP_LIMIT,
    )(block_scales, columns, live, blocks, y0)
    got_o, got_e = swap_o(to_o), swap_e(to_e)
    diag, sym, edge_t, base = call(first_local_kernel, [column, square, square, tall32], [VMEM] * 4, product, 10_000_000)(
        own, edge, onsite[:, None], y0
    )
    part = ((2 * B, K), BF16)
    sides = pltpu.VMEM((2, 2 * B, K), BF16)
    spare = [pltpu.VMEM((OWN, K), BF16), sides]
    edge, edge_t, y, *sends = call(
        first_post_kernel, [square, square, tall, part, part, part, part], [VMEM] * 7, 3 * product, 9_000_000, spare, {1: 0, 2: 1}
    )(base, edge, edge_t, to_e, to_o, got_e, got_o)
    older = y0
    got = exchange(*sends[:2])
    got2 = exchange(*sends[2:])
    for step in range(1, DEG):
        base = call(local_kernel, [tall32], [VMEM] * 4, product, 3_500_000)(sym, diag, y, older)[0]
        older = y
        if step < DEG - 1:
            outs = [tall, part, part]
            specs = [VMEM] * 6
            y, *sends = call(functools.partial(post_kernel, 0), outs, specs, 2 * product, 6_000_000, spare)(
                base, edge, edge_t, *got, y
            )
            got = exchange(*sends)
            y, *sends = call(functools.partial(post_kernel, 1), outs, specs, 2 * product, 6_000_000, spare)(
                base, edge, edge_t, *got2, y
            )
            got2 = exchange(*sends)
        else:
            y = call(last_first_kernel, [tall], [VMEM] * 5, product, 4_000_000, [sides])(base, edge, *got, y)[0]
            y, gram = call(last_kernel, [tall, ((K, K), F32)], [VMEM] * 5, product, 4_000_000, [sides])(base, edge, *got2, y)
    for stride, size in digits():
        gram = group_sum(gram, stride, size)
    scale = float(np.sqrt(total * B))
    return call(
        functools.partial(finish_kernel, scale), [tall32], [VMEM] * 2, 2 * product, 1_000_000, [pltpu.VMEM((K, K), F32)]
    )(gram, y)[0]


def solution(mesh):
    return jax.shard_map(
        local,
        mesh=mesh,
        in_specs=(
            P(AXES, None, None, None),
            P(AXES, None),
            P(AXES, None),
            P(AXES),
            P(AXES),
            P(AXES, None),
        ),
        out_specs=P(AXES, None),
        check_vma=False,
    )
```

```python
import functools

import jax
import jax.numpy as jnp
import numpy as np
from jax import lax
from jax.experimental import pallas as pl
from jax.experimental.pallas import tpu as pltpu
from jax.sharding import PartitionSpec as P

DEG = 5
B = 256
K = 128
ROWS = 4
OWN = ROWS * B
REACH = 4
SPAN = 2 * REACH + 1
AXES = ("row", "col")
ALPHA = 2.0 / 1.1
SHIFT = 0.2
F32 = jnp.float32
BF16 = jnp.bfloat16
EDGE = (8, 9, 2, 3)
TO_RIGHT = ((2, 10), (3, 10), (3, 11))
TO_LEFT = ((0, 0), (0, 1), (1, 1))
HANDED = 3 * 2 * B
T = 8


def rows(i, n=1):
    return pl.ds(i * B, n * B)


def dot(a, b):
    return jnp.dot(a, b, preferred_element_type=F32)


def read_block(ref, i):
    return jnp.concatenate([ref[rows(2 * i), :], ref[rows(2 * i + 1), :]], axis=1)


def flip(block):
    return block.astype(F32).T


def prep_kernel(total, scales_in, columns_in, live_in, blocks, y0, own_out, edge_out, to_e, to_o, buf, acc, own, edge, msg, y0_in, scales, columns, live, head, after, sem, sent):
    small = [
        pltpu.make_async_copy(source, target, sent.at[15 + i])
        for i, (source, target) in enumerate(((live_in, live), (columns_in, columns), (scales_in, scales)))
    ]
    for copy in small:
        copy.start()
    start_y0 = pltpu.make_async_copy(y0, y0_in, sent.at[12])
    start_y0.start()
    copies = [pltpu.make_async_copy(blocks.at[a], buf.at[a], sem.at[a]) for a in range(ROWS)]
    for copy in copies:
        copy.start()
    even = lax.rem(lax.axis_index(AXES), 2) == 0
    first = lax.axis_index(AXES) * ROWS
    for copy in small:
        copy.wait()
    for a in range(ROWS):
        for o in range(SPAN):
            head[a, o] = -1

        def chain(s, carry, a=a):
            o = lax.rem(columns[a, s] - (first + a) + REACH + total, total)
            after[a, s] = head[a, o]
            head[a, o] = s
            return carry

        lax.fori_loop(0, live[a], chain, 0)
    start_y0.wait()
    waits = []
    for i, target in enumerate((to_e, to_o)):
        copy = pltpu.make_async_copy(y0_in, target.at[pl.ds(HANDED + 2 * B, OWN), :], sent.at[10 + i])
        copy.start()
        waits.append(copy)
    turned = flip(y0_in[...]).astype(BF16)

    def post_message(right, start, count, slot):
        side = 0 if right else 1
        part = pl.ds(start, count)

        @pl.when(even == right)
        def _():
            pltpu.make_async_copy(msg.at[side, part, :], to_e.at[part, :], sent.at[slot]).start()

        @pl.when(even != right)
        def _():
            pltpu.make_async_copy(msg.at[side, part, :], to_o.at[part, :], sent.at[slot]).start()

        waits.append(pltpu.make_async_copy(msg.at[side, part, :], to_e.at[part, :], sent.at[slot]))

    def put(a, p, value):
        if 4 <= p < 8:
            own[rows(a), rows(p - 4)] = value
        elif p in EDGE:
            edge[rows(a), rows(EDGE.index(p))] = value
        else:
            side, places = (0, TO_RIGHT) if p > 8 else (1, TO_LEFT)
            i = places.index((a, p))
            msg[side, rows(2 * i), :] = value[:, :K]
            msg[side, rows(2 * i + 1), :] = value[:, K:]

    def scaled(a, s):
        return (scales[a, s] * ALPHA) * buf[a, s].astype(F32)

    def place(a, o):
        s = head[a, o]

        @pl.when(s < 0)
        def _():
            put(a, a + o, jnp.zeros((B, B), BF16))

        @pl.when(s >= 0)
        def _():
            rest = after[a, jnp.maximum(s, 0)]

            @pl.when(rest < 0)
            def _():
                put(a, a + o, scaled(a, s).astype(BF16))

            last = after[a, jnp.maximum(rest, 0)]

            @pl.when((rest >= 0) & (last < 0))
            def _():
                put(a, a + o, (scaled(a, s) + scaled(a, rest)).astype(BF16))

            @pl.when((rest >= 0) & (last >= 0))
            def _():
                acc[...] = scaled(a, s)

                def more(t):
                    acc[...] = acc[...] + scaled(a, t)
                    return after[a, t]

                lax.while_loop(lambda t: t >= 0, more, rest)
                put(a, a + o, acc[...].astype(BF16))

    edge[rows(0), rows(1)] = jnp.zeros((B, B), BF16)
    edge[rows(3), rows(2)] = jnp.zeros((B, B), BF16)
    for a in range(ROWS):
        copies[a].wait()
        for o in range(SPAN):
            place(a, o)
        for i, (source, target) in enumerate(((own, own_out), (edge, edge_out))):
            copy = pltpu.make_async_copy(source.at[rows(a), :], target.at[rows(a), :], sent.at[4 * i + a])
            copy.start()
            waits.append(copy)
        if a % 2 == 1:
            post_message(a == 3, 0, HANDED, 8 if a == 3 else 9)
    terms = dot(turned, edge[...]).T.astype(BF16)
    msg[0, pl.ds(HANDED, 2 * B), :] = terms[: 2 * B]
    msg[1, pl.ds(HANDED, 2 * B), :] = terms[2 * B :]
    post_message(True, HANDED, 2 * B, 13)
    post_message(False, HANDED, 2 * B, 14)
    for copy in waits:
        copy.wait()


def first_local_kernel(own, edge, onsite, y0, diag, sym, edge_t, base):
    for a in range(ROWS):
        for b in range(a + 1):
            value = own[rows(a), rows(b)].astype(F32) + flip(own[rows(b), rows(a)])
            sym[rows(a), rows(b)] = value.astype(BF16)
            if b < a:
                sym[rows(b), rows(a)] = value.T.astype(BF16)
    for a in range(ROWS):
        for j in range(4):
            edge_t[rows(j), rows(a)] = flip(edge[rows(a), rows(j)]).astype(BF16)
    diag[...] = ALPHA * (onsite[...] - SHIFT)
    base[...] = diag[...] * y0[...].astype(F32) + dot(sym[...], y0[...])


def by_parity(body):
    parity = lax.rem(lax.axis_index(AXES), 2)
    for value in (0, 1):

        @pl.when(parity == value)
        def _(even=value == 0):
            body(even)


def halo_right(a, edge, got, halo=0):
    wide = 1 if a == 0 else 2
    return dot(edge[rows(a), rows(0, wide)], got[pl.ds(halo, wide * B), :])


def halo_left(a, edge, got, halo=0):
    skip = 1 if a == ROWS - 1 else 0
    return dot(edge[rows(a), rows(2 + skip, 2 - skip)], got[pl.ds(halo + skip * B, (2 - skip) * B), :])


def terms_of(a, got_left, got_right, start=0):
    got = got_left if a < 2 else got_right
    return got[pl.ds(start + (a % 2) * B, B), :].astype(F32)


HALF = K // 2


def half_mask(half):
    lane = lax.broadcasted_iota(jnp.int32, (B, K), 1)
    return (lane < HALF) if half == 0 else (lane >= HALF)


def take(sides, got_e, got_o):
    parity = lax.rem(lax.axis_index(AXES), 2)
    sides[parity] = got_e[...]
    sides[1 - parity] = got_o[...]


def give(sides, send_e, send_o):
    parity = lax.rem(lax.axis_index(AXES), 2)
    send_e[...] = sides[parity]
    send_o[...] = sides[1 - parity]


def pack(half, edge_t, y, sides, spare):
    mine = half_mask(half)
    for a in range(ROWS):
        value = jnp.where(mine, y[rows(a), :].astype(F32), 0.0)
        spare[rows(a), :] = pltpu.roll(value, HALF, 1).astype(BF16)

    def put(side, i, row, terms):
        sides[side, rows(i), :] = jnp.where(mine, y[rows(row), :].astype(F32), terms).astype(BF16)

    put(0, 0, 2, dot(edge_t[rows(0), :], spare[...]))
    put(0, 1, 3, dot(edge_t[rows(1), rows(1, 3)], spare[rows(1, 3), :]))
    put(1, 0, 0, dot(edge_t[rows(2), rows(0, 3)], spare[rows(0, 3), :]))
    put(1, 1, 1, dot(edge_t[rows(3), :], spare[...]))


def first_post_kernel(base, edge_in, edge_t_in, to_e, to_o, got_e, got_o, edge, edge_t, y, send_e, send_o, spare, sides):
    edge[...] = edge_in[...]
    edge_t[...] = edge_t_in[...]

    def body(even):
        to_right, to_left = (to_e, to_o) if even else (to_o, to_e)
        got_right, got_left = (got_e, got_o) if even else (got_o, got_e)
        for i, (r, c) in enumerate(TO_LEFT):
            block = read_block(got_right, i).astype(F32)
            edge_t[rows(r), rows(c)] = (edge_t[rows(r), rows(c)].astype(F32) + block).astype(BF16)
            edge[rows(c), rows(r)] = (edge[rows(c), rows(r)].astype(F32) + block.T).astype(BF16)
        for i, (c, p) in enumerate(TO_RIGHT):
            block = read_block(got_left, i).astype(F32)
            r = p - 8
            edge_t[rows(c), rows(r)] = (edge_t[rows(c), rows(r)].astype(F32) + block).astype(BF16)
            edge[rows(r), rows(c)] = (edge[rows(r), rows(c)].astype(F32) + block.T).astype(BF16)
        halo = HANDED + 2 * B
        for a in range(ROWS):
            total = base[rows(a), :] + halo_right(a, edge, got_right, halo)
            total += halo_left(a, edge, got_left, halo + 2 * B) + terms_of(a, got_left, got_right, HANDED)
            for places, source, got, start in ((TO_LEFT, to_left, got_left, 0), (TO_RIGHT, to_right, got_right, 8)):
                for i, (row, p) in enumerate(places):
                    if row == a:
                        total += dot(read_block(source, i), got[pl.ds(halo + (p - start) * B, B), :])
            y[rows(a), :] = (0.5 * total).astype(BF16)
    by_parity(body)
    pack(0, edge_t, y, sides, spare)
    give(sides, send_e, send_o)


def second_pack_kernel(edge_t, y, send_e, send_o, spare, sides):
    pack(1, edge_t, y, sides, spare)
    give(sides, send_e, send_o)


def local_kernel(sym, diag, y, older, base):
    base[...] = diag[...] * y[...].astype(F32) - older[...].astype(F32) + dot(sym[...], y[...])


def receive(half, base, edge, got_e, got_o, y_in, y, sides):
    take(sides, got_e, got_o)
    right, left = sides.at[0], sides.at[1]
    for a in range(ROWS):
        total = base[rows(a), :] + halo_right(a, edge, right) + halo_left(a, edge, left)
        total += pltpu.roll(terms_of(a, left, right), HALF, 1)
        y[rows(a), :] = jnp.where(half_mask(half), total, y_in[rows(a), :].astype(F32)).astype(BF16)


def post_kernel(half, base, edge, edge_t, got_e, got_o, y_in, y, send_e, send_o, spare, sides):
    receive(half, base, edge, got_e, got_o, y_in, y, sides)
    pack(half, edge_t, y, sides, spare)
    give(sides, send_e, send_o)


def last_first_kernel(base, edge, got_e, got_o, y_in, y, sides):
    receive(0, base, edge, got_e, got_o, y_in, y, sides)


def last_kernel(base, edge, got_e, got_o, y_in, y, gram, sides):
    receive(1, base, edge, got_e, got_o, y_in, y, sides)
    gram[...] = lax.dot_general(y[...], y[...], (((0,), (0,)), ((), ())), preferred_element_type=F32)


def lane_fill(x, c):
    return jnp.take_along_axis(x, jnp.full((T, K), c, jnp.int32), axis=1)


def row_fill(x, j):
    return jnp.take_along_axis(x, jnp.full((T, K), j, jnp.int32), axis=0)


def inverse_factor(gram, inverse):
    count = K // T
    lane = lax.broadcasted_iota(jnp.int32, (T, K), 1)
    sub = lax.broadcasted_iota(jnp.int32, (T, K), 0)
    tiles = [gram[pl.ds(T * t, T), :] for t in range(count)]
    for k in range(count):
        first = T * k
        inside = (lane >= first) & (lane < first + T)
        spread = [lane_fill(tiles[k], first + c) for c in range(T)]
        rest = jnp.where(inside, 0.0, tiles[k])
        steps = []
        scale = jnp.zeros((T, K), F32)
        for j in range(T):
            pivot = row_fill(spread[j], j)
            inv = 1.0 / pivot
            ratios = {c: row_fill(spread[c], j) * inv for c in range(j + 1, T)}
            row = jnp.where(lane == first + j, 1.0, row_fill(rest, j)) * inv
            steps.append((ratios, row))
            rest = rest - jnp.where(sub > j, spread[j], 0.0) * row
            for c in range(j + 1, T):
                spread[c] = spread[c] - spread[j] * ratios[c]
            scale = jnp.where(sub == j, lax.rsqrt(pivot), scale)
        unit = jnp.where(lane < first + sub, rest, jnp.where(lane == first + sub, 1.0, 0.0))
        inverse[pl.ds(first, T), :] = unit * scale
        for t in range(k + 1, count):
            factors = [lane_fill(tiles[t], first + c) for c in range(T)]
            value = jnp.where(inside, 0.0, tiles[t])
            for j, (ratios, row) in enumerate(steps):
                value = value - factors[j] * row
                for c in range(j + 1, T):
                    factors[c] = factors[c] - factors[j] * ratios[c]
            tiles[t] = value


def finish_kernel(scale, gram, y, basis, inverse):
    inverse_factor(gram, inverse)
    value = inverse[...] * scale
    high = value.astype(BF16)
    low = (value - high.astype(F32)).astype(BF16)
    dims = (((1,), (1,)), ((), ()))
    basis[...] = lax.dot_general(y[...], high, dims, preferred_element_type=F32) + lax.dot_general(
        y[...], low, dims, preferred_element_type=F32
    )


VMEM = pl.BlockSpec(memory_space=pltpu.VMEM)
SMEM = pl.BlockSpec(memory_space=pltpu.SMEM)
HBM = pl.BlockSpec(memory_space=pltpu.HBM)
LIMIT = 20 * 1024 * 1024
PREP_LIMIT = 57 * 1000 * 1000


def call(kernel, outs, specs, flops, size, scratch=(), aliases=None, limit=LIMIT, out_spec=None):
    return pl.pallas_call(
        kernel,
        out_shape=[jax.ShapeDtypeStruct(*out) for out in outs],
        in_specs=list(specs),
        out_specs=[out_spec or VMEM] * len(outs),
        scratch_shapes=list(scratch),
        input_output_aliases=aliases or {},
        cost_estimate=pl.CostEstimate(flops=flops, bytes_accessed=size, transcendentals=0),
        compiler_params=pltpu.CompilerParams(vmem_limit_bytes=limit),
    )


def swap_o(value):
    count = lax.axis_size(AXES)
    return lax.ppermute(value, AXES, [(i, (i + 1 if i % 2 else i - 1) % count) for i in range(count)])


def swap_e(value):
    return lax.ppermute(value, AXES, [(i, i ^ 1) for i in range(lax.axis_size(AXES))])


def exchange(send_e, send_o):
    got_o = swap_o(send_o)
    return swap_e(send_e), got_o


def group_sum(value, stride, size):
    count = lax.axis_size(AXES)
    parts = [value]
    for step in range(1, size):
        pairs = []
        for i in range(count):
            digit = (i // stride) % size
            partner = digit ^ step if size & (size - 1) == 0 else (digit + step) % size
            pairs.append((i, i + (partner - digit) * stride))
        parts.append(lax.ppermute(value, AXES, pairs))
    return sum(parts[1:], parts[0])


def digits():
    out, stride = [], 1
    for axis, cut in (("col", 4), ("row", 2)):
        left = lax.axis_size(axis)
        while left > 1:
            size = cut if left % cut == 0 else left
            out.append((stride, size))
            stride *= size
            left //= size
            cut = left if axis == "row" else cut
    return out


def local(blocks, block_scales, columns, live, onsite, start_vectors):
    slots = columns.shape[1]
    total = ROWS * lax.axis_size(AXES)
    column = ((OWN, 1), F32)
    tall = ((OWN, K), BF16)
    tall32 = ((OWN, K), F32)
    square = ((OWN, OWN), BF16)
    message = ((HANDED + 2 * B + OWN, K), BF16)
    product = 2 * OWN * OWN * K

    y0 = start_vectors
    own, edge, to_e, to_o = call(
        functools.partial(prep_kernel, total),
        [square, square, message, message],
        [HBM] * 5,
        product,
        10_000_000,
        [
            pltpu.VMEM((ROWS, slots, B, B), BF16),
            pltpu.VMEM((B, B), F32),
            pltpu.VMEM((OWN, OWN), BF16),
            pltpu.VMEM((OWN, OWN), BF16),
            pltpu.VMEM((2, HANDED + 2 * B, K), BF16),
            pltpu.VMEM((OWN, K), BF16),
            pltpu.SMEM((ROWS, slots), F32),
            pltpu.SMEM((ROWS, slots), jnp.int32),
            pltpu.SMEM((ROWS,), jnp.int32),
            pltpu.SMEM((ROWS, SPAN), jnp.int32),
            pltpu.SMEM((ROWS, slots), jnp.int32),
            pltpu.SemaphoreType.DMA((ROWS,)),
            pltpu.SemaphoreType.DMA((18,)),
        ],
        out_spec=HBM,
        limit=PREP_LIMIT,
    )(block_scales, columns, live, blocks, y0)
    got_o, got_e = swap_o(to_o), swap_e(to_e)
    diag, sym, edge_t, base = call(first_local_kernel, [column, square, square, tall32], [VMEM] * 4, product, 10_000_000)(
        own, edge, onsite[:, None], y0
    )
    part = ((2 * B, K), BF16)
    sides = pltpu.VMEM((2, 2 * B, K), BF16)
    spare = [pltpu.VMEM((OWN, K), BF16), sides]
    edge, edge_t, y, *sends = call(
        first_post_kernel, [square, square, tall, part, part], [VMEM] * 7, 2 * product, 9_000_000, spare, {1: 0, 2: 1}
    )(base, edge, edge_t, to_e, to_o, got_e, got_o)
    older = y0
    got = exchange(*sends)
    got2 = exchange(*call(second_pack_kernel, [part, part], [VMEM] * 2, product, 3_000_000, spare)(edge_t, y))
    for step in range(1, DEG):
        base = call(local_kernel, [tall32], [VMEM] * 4, product, 3_500_000)(sym, diag, y, older)[0]
        older = y
        if step < DEG - 1:
            outs = [tall, part, part]
            specs = [VMEM] * 6
            y, *sends = call(functools.partial(post_kernel, 0), outs, specs, 2 * product, 6_000_000, spare)(
                base, edge, edge_t, *got, y
            )
            got = exchange(*sends)
            y, *sends = call(functools.partial(post_kernel, 1), outs, specs, 2 * product, 6_000_000, spare)(
                base, edge, edge_t, *got2, y
            )
            got2 = exchange(*sends)
        else:
            y = call(last_first_kernel, [tall], [VMEM] * 5, product, 4_000_000, [sides])(base, edge, *got, y)[0]
            y, gram = call(last_kernel, [tall, ((K, K), F32)], [VMEM] * 5, product, 4_000_000, [sides])(base, edge, *got2, y)
    places = digits()
    for stride, size in [places[i] for i in (2, 0, 1, 3)]:
        gram = group_sum(gram, stride, size)
    scale = float(np.sqrt(total * B))
    return call(
        functools.partial(finish_kernel, scale), [tall32], [VMEM] * 2, 2 * product, 1_000_000, [pltpu.VMEM((K, K), F32)]
    )(gram, y)[0]


def solution(mesh):
    return jax.shard_map(
        local,
        mesh=mesh,
        in_specs=(
            P(AXES, None, None, None),
            P(AXES, None),
            P(AXES, None),
            P(AXES),
            P(AXES),
            P(AXES, None),
        ),
        out_specs=P(AXES, None),
        check_vma=False,
    )
```
